256 devices in a mesh: dp: 32 (over y_hi, z, core), proto: 8 (over y_lo, x).
Axes of the slice: x: 4, y: 4 (y_hi: 2, y_lo: 2; y = y_hi * 2 + y_lo), z: 8, core: 2. Of those that a mesh axis runs over, the one named last changes fastest.
Arguments:
- student_feats: bfloat16 [8192, 256], P('dp'), may hold values from -8 to 8
- teacher_feats: bfloat16 [2048, 256], P('dp'), may hold values from -8 to 8
- prototypes: bfloat16 [131072, 256], P('proto'), may hold values from -0.5 to 0.5
- pairs: int32 [8192, 2], P('dp'), may hold values from 0 to 63
- pair_mask: int32 [8192, 2], P('dp'), may hold values 0 or 1
- epoch: int32 [1], replicated, may hold values from 0 to 30
Outputs:
- loss_rows: float32 [8192], P('dp')
- grad_feats: float32 [8192, 256], P('dp')
- grad_proto: float32 [131072, 256], P(('proto', 'dp'))
The draws below stay inside these ranges and needn't reach their ends.
Inputs may be any that keep to these rules, and one draw needn't show every extreme that they name: Entry p of row i names teacher crop (i // 256) * 64 + pairs[i, p].
All inputs are finite; a program needn't handle non-finite values. No bound on the sum of `pair_mask` on one device may be relied on, other than what follows from the above.
Results may differ from the reference program's by a relative error of at most 0.0027.
Values may be sent and summed in bfloat16 or wider, within the bound.
No kernel may reach another device: no remote copies, remote signals or barrier semaphores. Data moves between devices by JAX's collectives and lax.ppermute only.
A program may use at most 128 MiB of HBM per device.

```python
import jax
import jax.numpy as jnp
from jax import lax

BOTTLE = 256
PROTOS = 131072
CROPS_DEV = 256
TEACH_DEV = 64
ITERS = 3
CROPS = 8192
TEACH = 2048


cluster_count = 16


def shared_layout(key):
    base = jax.random.fold_in(key, 101)
    key_centre, key_cluster, key_level = jax.random.split(base, 3)
    block_count = TEACH // TEACH_DEV
    centres = jax.random.normal(key_centre, (cluster_count, BOTTLE), jnp.float32)
    block_clusters = jax.random.randint(key_cluster, (block_count, 2), 0, cluster_count)
    block_level = jax.random.uniform(key_level, (block_count,), jnp.float32, 0.0, 1.0)
    return (centres, block_clusters, block_level)


def cluster_rows(key, count, per_block, block_clusters):
    row_index = jnp.arange(count, dtype=jnp.int32)
    block_index = row_index // per_block
    second = (jax.random.randint(key, (count,), 0, 4) == 0).astype(jnp.int32)
    return (block_clusters[block_index, second], block_index)


def draw_teacher_feats(key, part):
    centres, block_clusters, block_level = shared_layout(key)
    key = jax.random.fold_in(key, 7)
    key_pick, key_noise = jax.random.split(key, 2)
    cluster_of, block_index = cluster_rows(key_pick, TEACH, TEACH_DEV, block_clusters)
    jitter = jax.random.normal(key_noise, (TEACH, BOTTLE), jnp.float32)
    amplitude = 0.8 + 1.4 * block_level[block_index]
    values = amplitude[:, None] * centres[cluster_of] + jitter
    return jnp.clip(values, -8.0, 8.0).astype(jnp.bfloat16)


def draw_student_feats(key, part):
    centres, block_clusters, block_level = shared_layout(key)
    key = jax.random.fold_in(key, 13)
    key_pick, key_noise = jax.random.split(key, 2)
    cluster_of, block_index = cluster_rows(key_pick, CROPS, CROPS_DEV, block_clusters)
    jitter = jax.random.normal(key_noise, (CROPS, BOTTLE), jnp.float32)
    amplitude = 0.6 + block_level[block_index]
    values = amplitude[:, None] * centres[cluster_of] + jitter
    return jnp.clip(values, -8.0, 8.0).astype(jnp.bfloat16)


def draw_prototypes(key, part):
    centres, block_clusters, block_level = shared_layout(key)
    key = jax.random.fold_in(key, 19)
    key_share, key_member, key_noise = jax.random.split(key, 3)
    row_index = jnp.arange(PROTOS, dtype=jnp.int32)
    region = row_index * cluster_count // PROTOS
    share_of = jax.random.randint(key_share, (cluster_count,), 10, 90)
    member = jax.random.randint(key_member, (PROTOS,), 0, 100) < share_of[region]
    jitter = jax.random.normal(key_noise, (PROTOS, BOTTLE), jnp.float32)
    strength = 1.5
    values = jnp.where(member[:, None], strength * centres[region], 0.0) + jitter
    return (jnp.clip(values, -8.0, 8.0) * 0.0625).astype(jnp.bfloat16)


def touch_ends(drawn, own_key, smallest, largest):
    longest = drawn.shape.index(max(drawn.shape))
    spots = []
    for shift in (0, 1):
        where = [jax.random.randint(jax.random.fold_in(own_key, axis), (), 0, length) for axis, length in enumerate(drawn.shape)]
        where[longest] = (where[longest] + shift) % drawn.shape[longest]
        spots.append(tuple(where))
    return drawn.at[spots[0]].set(smallest).at[spots[1]].set(largest)


def setup_inputs(seed: int = 0) -> dict:
    key_of = jax.random.split(jax.random.key(seed), 7)
    return {
        "student_feats": draw_student_feats(jax.random.fold_in(key_of[6], 71), 0),
        "teacher_feats": draw_teacher_feats(jax.random.fold_in(key_of[6], 71), 0),
        "prototypes": draw_prototypes(jax.random.fold_in(key_of[6], 71), 0),
        "pairs": touch_ends(jax.random.randint(key_of[3], (CROPS, 2), 0, TEACH_DEV), jax.random.fold_in(key_of[3], 1), 0, TEACH_DEV - 1).astype(jnp.int32),
        "pair_mask": touch_ends((jax.random.randint(key_of[4], (CROPS, 2), 0, 4) < 3).astype(jnp.int32), jax.random.fold_in(key_of[4], 1), 0, 1),
        "epoch": jax.random.randint(key_of[5], (1,), 0, 31).astype(jnp.int32),
    }


epsilon_norm = 1e-06
student_temp = 0.1
loss_scale = 256.0

def unit_rows(values):
    wide = values.astype(jnp.float32)
    inverse = lax.rsqrt(lax.optimization_barrier(jnp.sum(wide * wide, axis=1, keepdims=True)) + epsilon_norm)
    return (wide * inverse, inverse)

def reference(student_feats, teacher_feats, prototypes, pairs, pair_mask, epoch):
    block = min(4096, PROTOS)
    nblocks = PROTOS // block
    wn, inv_w = unit_rows(prototypes)
    wnb = wn.astype(jnp.bfloat16)
    w_blocks = wnb.reshape(nblocks, block, BOTTLE)
    wn_blocks = wn.reshape(nblocks, block, BOTTLE)
    inv_blocks = inv_w.reshape(nblocks, block, 1)
    zs, inv_s = unit_rows(student_feats)
    zsb = zs.astype(jnp.bfloat16)
    zt, unused = unit_rows(teacher_feats)
    ztb = zt.astype(jnp.bfloat16)
    tau_t = 0.04 + 0.001 * epoch[0].astype(jnp.float32)

    def teacher_codes(w_block, columns, row_list):
        codes = jnp.exp(jnp.dot(ztb, w_block.T, preferred_element_type=jnp.float32) / tau_t)
        for index in range(len(row_list)):
            codes = codes / columns[index][None, :]
            codes = codes / row_list[index][:, None]
        return codes
    col_hist = []
    row_hist = []
    for step in range(ITERS):

        def sweep(total, items):
            codes = teacher_codes(items[0], items[1:], row_hist)
            column = lax.optimization_barrier(jnp.sum(codes, axis=0))
            codes = codes / column[None, :]
            return (total + lax.optimization_barrier(jnp.sum(codes, axis=1)), column)
        rows_now, col_blocks = lax.scan(sweep, jnp.zeros((TEACH,), jnp.float32), (w_blocks,) + tuple(col_hist))
        col_hist.append(col_blocks)
        row_hist.append(rows_now)

    def expsum(total, w_block):
        logits = jnp.dot(zsb, w_block.T, preferred_element_type=jnp.float32) / student_temp
        return (total + lax.optimization_barrier(jnp.sum(jnp.exp(logits), axis=1)), 0)
    exp_total, unused_out = lax.scan(expsum, jnp.zeros((CROPS,), jnp.float32), w_blocks)
    log_total = jnp.log(exp_total)
    owner = (jnp.arange(CROPS, dtype=jnp.int32) // CROPS_DEV * TEACH_DEV).astype(jnp.int32)
    global_idx = pairs + owner[:, None]
    mask_f = pair_mask.astype(jnp.float32)
    msum = mask_f[:, 0] + mask_f[:, 1]

    def backward(carry, items):
        w_block, wn_block, inv_block = (items[0], items[1], items[2])
        codes = teacher_codes(w_block, items[3:], row_hist)
        qmix = codes[global_idx[:, 0]] * mask_f[:, 0:1] + codes[global_idx[:, 1]] * mask_f[:, 1:2]
        logits = jnp.dot(zsb, w_block.T, preferred_element_type=jnp.float32) / student_temp
        probs = jnp.exp(logits - log_total[:, None])
        dlogits = (loss_scale * (msum[:, None] * probs - qmix) / student_temp).astype(jnp.bfloat16)
        gz = carry[0] + jnp.dot(dlogits, w_block, preferred_element_type=jnp.float32)
        cross = carry[1] + lax.optimization_barrier(jnp.sum(qmix * logits, axis=1))
        gw = jnp.dot(dlogits.T, zsb, preferred_element_type=jnp.float32)
        grad = (gw - wn_block * lax.optimization_barrier(jnp.sum(wn_block * gw, axis=1, keepdims=True))) * inv_block
        return ((gz, cross), grad)
    start = (jnp.zeros((CROPS, BOTTLE), jnp.float32), jnp.zeros((CROPS,), jnp.float32))
    (gz, cross), grads = lax.scan(backward, start, (w_blocks, wn_blocks, inv_blocks) + tuple(col_hist))
    loss_rows = msum * log_total - cross
    grad_feats = (gz - zs * lax.optimization_barrier(jnp.sum(zs * gz, axis=1, keepdims=True))) * inv_s
    grad_proto = grads.reshape(PROTOS, BOTTLE)
    return (loss_rows, grad_feats, grad_proto)
```

```python
import jax
import jax.numpy as jnp
from jax import lax
from jax.experimental import pallas as pl
from jax.experimental.pallas import tpu as pltpu
from jax.sharding import Mesh, PartitionSpec as P

F32, BF16 = jnp.float32, jnp.bfloat16
YH, Z, C, YL, X = 2, 8, 2, 2, 4
NP = YL * X
D = 256
CR = 256
TE = 64
NT = YH * Z * C * TE
SH = 512
EPS = 1e-6
LOG2E = 1.4426950408889634
STUDENT = 10.0
SCALE = 2560.0
MIB = 1 << 20
NS = 4
CWS = 4


def dot(a, b, ca=1, cb=0, precision=None):
    return lax.dot_general(
        a, b, (((ca,), (cb,)), ((), ())), preferred_element_type=F32, precision=precision
    )


def unit(values):
    wide = values.astype(F32)
    inv = lax.rsqrt(jnp.sum(wide * wide, axis=1, keepdims=True) + EPS)
    return wide * inv, inv


def params(mib):
    return pltpu.CompilerParams(vmem_limit_bytes=mib * MIB, dimension_semantics=("arbitrary",))


def hbm(x):
    return pltpu.with_memory_space_constraint(x, pltpu.HBM)


ANY = pl.BlockSpec(memory_space=pl.ANY)


def call(body, idx, grid, ins, in_specs, outs, out_specs, scratch=(), mib=24, flops=0, nbytes=0, alias={}):
    return pl.pallas_call(
        body,
        grid_spec=pltpu.PrefetchScalarGridSpec(
            num_scalar_prefetch=1,
            grid=(grid,),
            in_specs=in_specs,
            out_specs=out_specs,
            scratch_shapes=list(scratch),
        ),
        out_shape=outs,
        compiler_params=params(mib),
        input_output_aliases=alias,
        cost_estimate=pl.CostEstimate(flops=flops, bytes_accessed=nbytes, transcendentals=0),
    )(idx, *ins)


def whole(shape):
    zeros = (0,) * len(shape)
    return pl.BlockSpec(shape, lambda i, s: zeros)


def spec(shape, fn):
    return pl.BlockSpec(shape, fn)


def sds(shape, dtype):
    return jax.ShapeDtypeStruct(shape, dtype)


def selector(pairs, mask):
    rows = lax.broadcasted_iota(jnp.int32, (TE, CR), 0)
    m = mask[...].astype(F32)
    return jnp.where(pairs[0:1, :] == rows, m[0:1, :], 0.0) + jnp.where(
        pairs[1:2, :] == rows, m[1:2, :], 0.0
    )


def prep_body(s, sf, tf, pairs, mask, spay, trep):
    zs, _ = unit(sf[...])
    spay[0:CR, :] = sf[...]
    spay[CR : CR + TE, :] = dot(selector(pairs, mask).astype(BF16), zs.astype(BF16)).astype(BF16)
    zt, _ = unit(tf[...])
    ztb = zt.astype(BF16)
    for b in range(YH * Z):
        trep[b] = ztb


def norm_body(s, w, after, out, done):
    for j in range(NS):
        wn, _ = unit(w[j, 0])
        out[j] = wn.astype(BF16)
    done[...] = jnp.zeros_like(done)


def e_step(w_chunks, z_refs, zs, zsb, g, tacc):
    i = pl.program_id(0)

    @pl.when(i == 0)
    def _():
        g[...] = jnp.zeros_like(g)
        tacc[...] = jnp.zeros_like(tacc)
        for q, blk in enumerate(z_refs):
            zq, _ = unit(blk[0:CR, :])
            zs[q * CR : (q + 1) * CR, :] = zq
            zsb[q * CR : (q + 1) * CR, :] = zq.astype(BF16)

    for wb in w_chunks:
        for q in range(2):
            rows = pl.ds(q * CR, CR)
            e = jnp.exp2(dot(zsb[rows, :], wb, 1, 1) * (STUDENT * LOG2E))
            t = e[:, 0:128]
            for k in range(1, SH // 128):
                t = t + e[:, k * 128 : (k + 1) * 128]
            tacc[rows, :] += t
            g[rows, :] += dot(e.astype(BF16), wb)


def e_last(s, yy, zs, g, tacc, out, trow):
    yh, c = s[0], s[2]
    for q in range(2):
        rows = pl.ds(q * CR, CR)
        zq, gq = zs[rows, :], g[rows, :]
        out[q * CR : (q + 1) * CR, :] = gq - zq * jnp.sum(zq * gq, axis=1, keepdims=True)
        t = jnp.sum(tacc[q * CR : (q + 1) * CR, :].T, axis=0, keepdims=True)
        trow[pl.ds((yh ^ yy) * 2 + (c ^ q), 1), :] = t


def e1_body(s, w, b00, b01, mask, keep, trow, zsb, wnb, zs, g, tacc):
    chunks = []
    for j in range(2):
        wn, _ = unit(w[j, 0])
        wb = wn.astype(BF16)
        wnb[j] = wb
        chunks.append(wb)
    e_step(chunks, (b00, b01), zs, zsb, g, tacc)

    @pl.when(pl.program_id(0) == pl.num_programs(0) - 1)
    def _():
        trow[...] = jnp.zeros_like(trow)
        e_last(s, 0, zs, g, tacc, keep, trow)
        m = mask[...].astype(F32)
        trow[pl.ds(s[0] * 2 + s[2] + 8, 1), :] = (m[0:1, :] + m[1:2, :]) * (1.0 / NP)


def e2_body(s, w, b10, b11, trow1, send, trow, zsb, zs, g, tacc):
    e_step([w[0], w[1]], (b10, b11), zs, zsb, g, tacc)

    @pl.when(pl.program_id(0) == pl.num_programs(0) - 1)
    def _():
        trow[...] = trow1[...]
        e_last(s, 1, zs, g, tacc, send, trow)
        send[2 * CR : 2 * CR + 16, :] = trow[...]


def put_rows(racc, rsc):
    for k in range(8):
        rsc[k : k + 1, :] = racc[0:1, k * 256 : (k + 1) * 256]


def k_body(s, w, za, zb, epoch, after, kt, rz, racc, rsc):
    i = pl.program_id(0)

    @pl.when(i == 0)
    def _():
        racc[...] = jnp.zeros_like(racc)

    tau = 0.04 + 0.001 * epoch[0:1, 0:1].astype(F32)
    factor = LOG2E / tau
    wn, _ = unit(w[...])
    wb = wn.astype(BF16)
    half = NT // 2
    ka = jnp.exp2(dot(wb, za[...], 1, 1) * factor)
    kb = jnp.exp2(dot(wb, zb[...], 1, 1) * factor)
    kt[:, 0:half] = ka
    kt[:, half:NT] = kb
    c = 1.0 / (jnp.sum(ka, axis=1, keepdims=True) + jnp.sum(kb, axis=1, keepdims=True))
    racc[0:1, 0:half] += jnp.sum(ka * c, axis=0, keepdims=True)
    racc[0:1, half:NT] += jnp.sum(kb * c, axis=0, keepdims=True)

    @pl.when(i == pl.num_programs(0) - 1)
    def _():
        put_rows(racc, rsc)
        for b in range(Z):
            rz[b] = rsc[...]


def mid1_body(s, rz, tpk, tin, after, out):
    r = jnp.sum(rz[...], axis=0)
    ab = tpk[...] + tin[2 * CR : 2 * CR + 16, :]
    for b in range(C * NP):
        out[b, 0:8, :] = r
        out[b, 8:12, :] = ab[0:4]
        out[b, 12:16, :] = ab[8:12]


def mid2_body(s, rz, keep, tin, gwp, out, same, g):
    c = s[2]
    r = jnp.sum(rz[...], axis=0)
    g[...] = keep[...] + tin[0 : 2 * CR, :]
    for cd in range(C):
        for p in range(NP):
            out[cd * NP + p, 0:8, :] = r
            out[cd * NP + p, 8:40, :] = g[pl.ds((c ^ cd) * CR + p * 32, 32), :]


def row_total(s, got, sc):
    c = s[2]
    same = jnp.zeros((8, D), F32)
    other = jnp.zeros((8, D), F32)
    for p in range(NP):
        same = same + got[c * NP + p, 0:8, :]
        other = other + got[(1 - c) * NP + p, 0:8, :]
    sc[0:4, :] = same[0:4] + other[4:8]
    sc[4:8, :] = same[4:8] + other[0:4]


def scales(s, got, rsc, u):
    row_total(s, got, rsc)
    inv = 1.0 / rsc[...]
    for k in range(8):
        u[0:1, k * 256 : (k + 1) * 256] = inv[k : k + 1, :]


def it2_body(s, kt, got, rz, racc, rsc, u):
    i = pl.program_id(0)

    @pl.when(i == 0)
    def _():
        racc[...] = jnp.zeros_like(racc)
        scales(s, got, rsc, u)

    k = kt[...]
    c = 1.0 / jnp.sum(k * u[...], axis=1, keepdims=True)
    racc[...] += jnp.sum(k * c, axis=0, keepdims=True)

    @pl.when(i == pl.num_programs(0) - 1)
    def _():
        put_rows(racc, rsc)
        for b in range(Z):
            rz[b] = rsc[...]


def it3_body(s, kt, got, rz, ccol, racc, rsc, u, crow):
    i = pl.program_id(0)

    @pl.when(i == 0)
    def _():
        racc[...] = jnp.zeros_like(racc)
        crow[...] = jnp.zeros_like(crow)
        scales(s, got, rsc, u)

    k = kt[...]
    ku = k * u[...]
    t = ku[:, 0:128]
    for j in range(1, NT // 128):
        t = t + ku[:, j * 128 : (j + 1) * 128]
    c = 1.0 / jnp.sum(t, axis=1, keepdims=True)
    ccol[...] = jnp.broadcast_to(c, ccol.shape)
    crow[pl.ds(i, 1), :] = 1.0 / jnp.sum(t.T, axis=0, keepdims=True)
    racc[...] += jnp.sum(k * c, axis=0, keepdims=True)

    @pl.when(i == pl.num_programs(0) - 1)
    def _():
        put_rows(racc, rsc)
        for b in range(Z):
            rz[b, 0:8, :] = rsc[...]
            rz[b, 8:16, :] = crow[...]


def gw_body(s, w, za, zb, got, after, out, a):
    yh, c = s[0], s[2]

    @pl.when(pl.program_id(0) == 0)
    def _():
        tot = jnp.sum(got[:, 8:16, :], axis=0)
        a[0:4, :] = tot[4:8] / tot[0:4]
        a[4:8, :] = tot[4:8]

    for j in range(2):
        wb = w[j]
        acc = None
        for q in range(4):
            zq = (za, zb)[q // 2][(q % 2) * CR : (q % 2 + 1) * CR, :]
            at = (yh ^ (q // 2)) * 2 + (c ^ (q % 2))
            e = jnp.exp2(dot(wb, zq, 1, 1) * (STUDENT * LOG2E)) * a[pl.ds(at, 1), :]
            part = dot(e.astype(BF16), zq)
            acc = part if acc is None else acc + part
        out[j] = acc


def cw_body(s, w, za, zb, epoch, rz, keep, send, zp, acc):
    i = pl.program_id(0)
    c = s[2]

    @pl.when(i == 0)
    def _():
        zp[0:TE, :] = za[...]
        zp[TE : 2 * TE, :] = zb[...]
        acc[...] = jnp.zeros_like(acc)

    factor = LOG2E / (0.04 + 0.001 * epoch[0:1, 0:1].astype(F32))
    part = None
    for j in range(CWS):
        wb = w[j]
        e = jnp.exp2(dot(zp[...], wb, 1, 1) * factor)
        at = i * CWS + j
        yy, zz = at // Z, at % Z
        for h in range(2):
            row = rz[zz, pl.ds(8 + 2 * yy + h, 1), :]
            codes = (e[:, h * 256 : (h + 1) * 256] * row).astype(BF16)
            one = dot(codes, wb[h * 256 : (h + 1) * 256])
            part = one if part is None else part + one
    acc[...] += part

    @pl.when(i == pl.num_programs(0) - 1)
    def _():
        r = jnp.sum(rz[:, 0:8, :], axis=0)
        keep[0:8, :] = r
        keep[8 : 8 + TE, :] = acc[0:TE, :]
        send[0:4, :] = r[4:8]
        send[4:8, :] = r[0:4]
        send[8 : 8 + TE, :] = acc[TE : 2 * TE, :]


def mid3_body(s, keep, tin, got2, out):
    pack = keep[...] + tin[...]
    g = jnp.sum(got2[:, 8:40, :], axis=0)
    for p in range(NP):
        out[p, 0:72, :] = pack
        out[p, 72:104, :] = g


def feats_body(s, sf, pairs, mask, got1, got3, loss, grad, rsc, trow, g):
    yh, z, c = s[0], s[1], s[2]
    zs, inv = unit(sf[...])
    zsb = zs.astype(BF16).astype(F32)
    trow[...] = jnp.sum(got1[:, 8:16, :], axis=0)
    at = yh * 2 + c
    t = trow[pl.ds(at, 1), :]
    msum = trow[pl.ds(at + 4, 1), :]
    a = jnp.broadcast_to(msum / t, (128, CR)).T[:, 0:1]
    rsc[...] = 1.0 / jnp.sum(got3[:, 0:8, :], axis=0)
    own = yh * Z + z
    row = rsc[pl.ds(own // 4, 1), :]
    u = row[:, 0:128]
    u = jnp.where(own % 4 >= 2, row[:, 128:256], u)
    col = jnp.broadcast_to(u, (128, 128)).T
    ucol = jnp.where(own % 2 == 1, col[TE : 2 * TE, 0:1], col[0:TE, 0:1])
    cw = jnp.sum(got3[:, 8:72, :], axis=0) * ucol
    for p in range(NP):
        g[p * 32 : (p + 1) * 32, :] = got3[p, 72:104, :]
    q = dot(selector(pairs, mask), cw, 0, 0, lax.Precision.HIGHEST)
    cross = dot(jnp.ones((8, D), F32), zsb * q, 1, 1, lax.Precision.HIGHEST)
    loss[...] = msum * jnp.log(t) - STUDENT * cross[0:1, :]
    gz = SCALE * (a * g[...] - q)
    grad[...] = (gz - zs * jnp.sum(zs * gz, axis=1, keepdims=True)) * inv


def proto_body(s, kt, ccol, h, gwp, w, got3, out, hsc):
    @pl.when(pl.program_id(0) == 0)
    def _():
        for k in range(8):
            for j in range(4):
                at = k * 4 + j
                hsc[at * TE : (at + 1) * TE, :] = h[(k % 2) * 4 + j, pl.ds((k // 2) * TE, TE), :]

    u = 1.0 / jnp.sum(got3[:, 0:8, :], axis=0)
    acc = None
    for k in range(8):
        cols = slice(k * 256, (k + 1) * 256)
        part = dot((kt[:, cols] * u[k : k + 1, :]).astype(BF16), hsc[cols, :])
        acc = part if acc is None else acc + part
    wn, inv = unit(w[...])
    gw = SCALE * (gwp[...] - acc * ccol[:, 0:1])
    out[...] = (gw - wn * jnp.sum(wn * gw, axis=1, keepdims=True)) * inv


def local(student, teacher, prototypes, pairs, mask, epoch):
    yh, z, c = lax.axis_index("yh"), lax.axis_index("z"), lax.axis_index("c")
    p = lax.axis_index(("yl", "x"))
    idx = jnp.stack([yh, z, c, p]).astype(jnp.int32)
    ep = epoch.reshape(1, 1)
    student, teacher, protos = hbm(student), hbm(teacher), hbm(prototypes)
    pairs, mask = hbm(pairs.T), hbm(mask.T)
    chunked = hbm(prototypes.reshape(YH * Z, C, SH, D))
    swap = [(0, 1), (1, 0)]
    prc = ("c", "yl", "x")

    spay, trep = call(
        prep_body, idx, 1,
        (student, teacher, pairs, mask),
        [whole((CR, D)), whole((TE, D)), whole((2, CR)), whole((2, CR))],
        [sds((CR + TE, D), BF16), sds((YH * Z, TE, D), BF16)],
        [whole((CR + TE, D)), whole((YH * Z, TE, D))],
        nbytes=1 << 20,
    )
    b00 = spay
    b01 = lax.ppermute(b00, "c", swap)
    b10 = lax.ppermute(b00, "yh", swap)
    b11 = lax.ppermute(b01, "yh", swap)
    za = lax.all_to_all(trep, ("yh", "z"), 0, 0, tiled=True).reshape(NT // 2, D)
    zb = lax.ppermute(za, "c", swap)
    first = yh == 0
    h_low = [jnp.where(first, a[CR:], b[CR:]) for a, b in ((b00, b10), (b01, b11))]
    h_high = [jnp.where(first, b[CR:], a[CR:]) for a, b in ((b00, b10), (b01, b11))]
    h4 = jnp.concatenate([h_low[0], h_high[0], h_low[1], h_high[1]], axis=0)
    hall = lax.all_gather(h4, "z", axis=0, tiled=False)

    steps = Z // 2
    pair_spec = spec((2, SH, D), lambda i, s: (i, 0, 0))
    pool = [pltpu.VMEM((2 * CR, D), F32), pltpu.VMEM((2 * CR, D), F32), pltpu.VMEM((2 * CR, 128), F32)]
    keep, trow1, zsa, wnb = call(
        e1_body, idx, steps,
        (chunked, b00, b01, mask),
        [spec((2, 1, SH, D), lambda i, s: (s[0] * steps + i, s[2], 0, 0))]
        + [whole((CR + TE, D))] * 2
        + [whole((2, CR))],
        [
            sds((2 * CR, D), F32), sds((16, D), F32),
            sds((2 * CR, D), BF16), pltpu.HBM((Z, SH, D), BF16),
        ],
        [whole((2 * CR, D)), whole((16, D)), whole((2 * CR, D)), pair_spec],
        pool, flops=4 << 30, nbytes=4 << 20,
    )
    send, tpk, zsc = call(
        e2_body, idx, steps,
        (hbm(wnb), b10, b11, trow1),
        [pair_spec] + [whole((CR + TE, D))] * 2 + [whole((16, D))],
        [sds((2 * CR + 16, D), F32), sds((16, D), F32), sds((2 * CR, D), BF16)],
        [whole((2 * CR + 16, D)), whole((16, D)), whole((2 * CR, D))],
        pool, flops=4 << 30, nbytes=4 << 20,
    )
    tin = lax.ppermute(send, "yh", swap)

    rows = 256
    per = SH // rows
    ksteps = YH * per
    kt, rz1 = call(
        k_body, idx, ksteps,
        (protos, za, zb, ep, tpk),
        [
            spec((rows, D), lambda i, s: ((((i // per) * Z + s[1]) * C + s[2]) * per + i % per, 0)),
            whole((NT // 2, D)), whole((NT // 2, D)), whole((1, 1)), ANY,
        ],
        [pltpu.HBM((YH * SH, NT), F32), sds((Z, 8, D), F32)],
        [spec((rows, NT), lambda i, s: (i, 0)), whole((Z, 8, D))],
        [pltpu.VMEM((1, NT), F32), pltpu.VMEM((8, D), F32)],
        flops=4 << 30, nbytes=10 << 20,
    )
    wnc, done = call(
        norm_body, idx, YH * Z // NS,
        (chunked, rz1),
        [spec((NS, 1, SH, D), lambda i, s: (i, s[2], 0, 0)), ANY],
        [pltpu.HBM((YH * Z, SH, D), BF16), sds((8, 128), F32)],
        [spec((NS, SH, D), lambda i, s: (i, 0, 0)), whole((8, 128))],
        flops=2 << 30, nbytes=8 << 20,
    )
    rz1 = lax.all_to_all(rz1, "z", 0, 0, tiled=True)
    pay1 = call(
        mid1_body, idx, 1,
        (rz1, tpk, tin, done),
        [whole((Z, 8, D)), whole((16, D)), whole((2 * CR + 16, D)), ANY],
        sds((C * NP, 16, D), F32), whole((C * NP, 16, D)),
        nbytes=1 << 19,
    )
    got1 = lax.all_to_all(pay1, prc, 0, 0, tiled=True)

    it_scratch = [pltpu.VMEM((1, NT), F32), pltpu.VMEM((8, D), F32), pltpu.VMEM((1, NT), F32)]
    kt_spec = spec((rows, NT), lambda i, s: (i, 0))
    rz2 = call(
        it2_body, idx, ksteps,
        (hbm(kt), got1),
        [kt_spec, whole((C * NP, 16, D))],
        sds((Z, 8, D), F32), whole((Z, 8, D)),
        it_scratch, nbytes=9 << 20,
    )
    gwp, ratio = call(
        gw_body, idx, steps,
        (hbm(wnb), zsa, zsc, got1, rz2),
        [pair_spec, whole((2 * CR, D)), whole((2 * CR, D)), whole((C * NP, 16, D)), ANY],
        [pltpu.HBM((Z, SH, D), F32), sds((8, D), F32)],
        [pair_spec, whole((8, D))],
        flops=8 << 30, nbytes=8 << 20,
    )
    rz2 = lax.all_to_all(rz2, "z", 0, 0, tiled=True)
    pay2, gwp = call(
        mid2_body, idx, 1,
        (rz2, keep, tin, hbm(gwp)),
        [whole((Z, 8, D)), whole((2 * CR, D)), whole((2 * CR + 16, D)), ANY],
        [sds((C * NP, 40, D), F32), pltpu.HBM((Z, SH, D), F32)], [whole((C * NP, 40, D)), ANY],
        [pltpu.VMEM((2 * CR, D), F32)],
        nbytes=2 << 20, alias={4: 1},
    )
    gwp = lax.psum_scatter(gwp, "z", scatter_dimension=0, tiled=False)
    got2 = lax.all_to_all(pay2, prc, 0, 0, tiled=True)
    rz3, ccol = call(
        it3_body, idx, ksteps,
        (hbm(kt), got2),
        [kt_spec, whole((C * NP, 40, D))],
        [sds((Z, 16, D), F32), pltpu.HBM((YH * SH, 128), F32)],
        [whole((Z, 16, D)), spec((rows, 128), lambda i, s: (i, 0))],
        it_scratch + [pltpu.VMEM((8, D), F32)], nbytes=9 << 20,
    )
    rz3 = lax.all_to_all(rz3, "z", 0, 0, tiled=True)
    keep3, send3 = call(
        cw_body, idx, YH * Z // CWS,
        (hbm(wnc), za, zb, ep, rz3),
        [
            spec((CWS, SH, D), lambda i, s: (i, 0, 0)),
            spec((TE, D), lambda i, s: (s[0] * Z + s[1], 0)),
            spec((TE, D), lambda i, s: (s[0] * Z + s[1], 0)),
            whole((1, 1)), whole((Z, 16, D)),
        ],
        [sds((8 + TE, D), F32)] * 2, [whole((8 + TE, D))] * 2,
        [pltpu.VMEM((2 * TE, D), BF16), pltpu.VMEM((2 * TE, D), F32)],
        flops=1 << 30, nbytes=6 << 20,
    )
    tin3 = lax.ppermute(send3, "c", swap)
    pay3 = call(
        mid3_body, idx, 1,
        (keep3, tin3, got2),
        [whole((8 + TE, D))] * 2 + [whole((C * NP, 40, D))],
        sds((NP, 104, D), F32), whole((NP, 104, D)),
        nbytes=2 << 20,
    )
    got3 = lax.all_to_all(pay3, ("yl", "x"), 0, 0, tiled=True)

    loss, grad_feats = call(
        feats_body, idx, 1,
        (student, pairs, mask, got1, got3),
        [whole((CR, D)), whole((2, CR)), whole((2, CR)), whole((C * NP, 16, D)), whole((NP, 104, D))],
        [sds((1, CR), F32), sds((CR, D), F32)],
        [whole((1, CR)), whole((CR, D))],
        [pltpu.VMEM((8, D), F32), pltpu.VMEM((8, D), F32), pltpu.VMEM((CR, D), F32)],
        nbytes=2 << 20,
    )
    part = SH // 4
    row_spec = lambda lanes: spec((part, lanes), lambda i, s: (s[0] * 4 + i, 0))
    grad_proto = call(
        proto_body, idx, 4,
        (hbm(kt), hbm(ccol), hbm(hall), hbm(gwp), protos, got3),
        [
            row_spec(NT), row_spec(128), whole((Z, 4 * TE, D)),
            spec((part, D), lambda i, s: (i, 0)),
            spec((part, D), lambda i, s: (((s[0] * Z + s[1]) * C + s[2]) * 4 + i, 0)),
            whole((NP, 104, D)),
        ],
        sds((SH, D), F32), spec((part, D), lambda i, s: (i, 0)),
        [pltpu.VMEM((NT, D), BF16)],
        flops=1 << 29, nbytes=8 << 20,
    )
    return loss.reshape(CR), grad_feats, grad_proto


def solution(mesh):
    fine = Mesh(mesh.devices.reshape(YH, Z, C, YL, X), ("yh", "z", "c", "yl", "x"))
    dp, proto = ("yh", "z", "c"), ("yl", "x")
    in_specs = (P(dp, None), P(dp, None), P(proto, None), P(dp, None), P(dp, None), P())
    out_specs = (P(dp), P(dp, None), P(proto + dp, None))
    return jax.shard_map(local, mesh=fine, in_specs=in_specs, out_specs=out_specs, check_vma=False)
```

```python
import jax
import jax.numpy as jnp
from jax import lax
from jax.experimental import pallas as pl
from jax.experimental.pallas import tpu as pltpu
from jax.sharding import Mesh, PartitionSpec as P

F32, BF16 = jnp.float32, jnp.bfloat16
YH, Z, C, YL, X = 2, 8, 2, 2, 4
NP = YL * X
D = 256
CR = 256
TE = 64
NT = YH * Z * C * TE
SH = 512
EPS = 1e-6
LOG2E = 1.4426950408889634
STUDENT = 10.0
SCALE = 2560.0
MIB = 1 << 20
KC, KR = 4, 256
CWS = 8


def dot(a, b, ca=1, cb=0, precision=None):
    return lax.dot_general(
        a, b, (((ca,), (cb,)), ((), ())), preferred_element_type=F32, precision=precision
    )


def unit(values):
    wide = values.astype(F32)
    inv = lax.rsqrt(jnp.sum(wide * wide, axis=1, keepdims=True) + EPS)
    return wide * inv, inv


def params(mib):
    return pltpu.CompilerParams(vmem_limit_bytes=mib * MIB, dimension_semantics=("arbitrary",))


def hbm(x):
    return pltpu.with_memory_space_constraint(x, pltpu.HBM)


ANY = pl.BlockSpec(memory_space=pl.ANY)


def call(body, idx, grid, ins, in_specs, outs, out_specs, scratch=(), mib=24, flops=0, nbytes=0, alias={}):
    return pl.pallas_call(
        body,
        grid_spec=pltpu.PrefetchScalarGridSpec(
            num_scalar_prefetch=1,
            grid=(grid,),
            in_specs=in_specs,
            out_specs=out_specs,
            scratch_shapes=list(scratch),
        ),
        out_shape=outs,
        compiler_params=params(mib),
        input_output_aliases=alias,
        cost_estimate=pl.CostEstimate(flops=flops, bytes_accessed=nbytes, transcendentals=0),
    )(idx, *ins)


def loop(n, body):
    lax.fori_loop(0, n, lambda k, x: (body(k), x)[1], 0)


def copier(source, target, sem):
    return lambda k: pltpu.make_async_copy(source(k), target(k), sem.at[k])


def start_all(n, copy):
    loop(n, lambda k: copy(k).start())


def wait_all(n, copy):
    loop(n, lambda k: copy(k).wait())


def sems(n):
    return pltpu.SemaphoreType.DMA((n,))


def whole(shape):
    zeros = (0,) * len(shape)
    return pl.BlockSpec(shape, lambda i, s: zeros)


def spec(shape, fn):
    return pl.BlockSpec(shape, fn)


def sds(shape, dtype):
    return jax.ShapeDtypeStruct(shape, dtype)


def selector(pairs, mask):
    rows = lax.broadcasted_iota(jnp.int32, (TE, CR), 0)
    m = mask[...].astype(F32)
    return jnp.where(pairs[0:1, :] == rows, m[0:1, :], 0.0) + jnp.where(
        pairs[1:2, :] == rows, m[1:2, :], 0.0
    )


def prep_body(s, sf, tf, pairs, mask, spay, trep):
    zs, _ = unit(sf[...])
    zsb = zs.astype(BF16)
    spay[0:CR, :] = zsb
    spay[CR : CR + TE, :] = dot(selector(pairs, mask).astype(BF16), zsb).astype(BF16)
    zt, _ = unit(tf[...])
    ztb = zt.astype(BF16)
    for b in range(YH * Z):
        trep[b] = ztb


def norm_body(s, w, after, out, done, wv, nv, si, so):
    n = YH * Z
    ins = copier(lambda j: w.at[j, s[2]], lambda j: wv.at[j], si)
    outs = copier(lambda j: nv.at[j], lambda j: out.at[j], so)
    start_all(n, ins)

    def step(j):
        ins(j).wait()
        wn, _ = unit(wv[j])
        nv[j] = wn.astype(BF16)
        outs(j).start()

    loop(n, step)
    done[...] = jnp.zeros_like(done)
    wait_all(n, outs)


def e_step(wb, z_refs, g, tacc):
    for q in range(2):
        rows = slice(q * CR, (q + 1) * CR)
        e = jnp.exp2(dot(z_refs[q][0:CR, :], wb, 1, 1) * (STUDENT * LOG2E))
        t = e[:, 0:128]
        for k in range(1, SH // 128):
            t = t + e[:, k * 128 : (k + 1) * 128]
        tacc[rows, :] += t
        g[rows, :] += dot(e.astype(BF16), wb)


def put_totals(s, yy, tacc, trow):
    yh, c = s[0], s[2]
    for q in range(2):
        t = jnp.sum(tacc[q * CR : (q + 1) * CR, :].T, axis=0, keepdims=True)
        trow[pl.ds((yh ^ yy) * 2 + (c ^ q), 1), :] = t


def e1_body(s, w, b00, b01, mask, keep, trow, wnb, tacc):
    @pl.when(pl.program_id(0) == 0)
    def _():
        keep[...] = jnp.zeros_like(keep)
        tacc[...] = jnp.zeros_like(tacc)

    for j in range(2):
        wn, _ = unit(w[j, 0])
        wb = wn.astype(BF16)
        wnb[j] = wb
        e_step(wb, (b00, b01), keep, tacc)

    @pl.when(pl.program_id(0) == pl.num_programs(0) - 1)
    def _():
        trow[...] = jnp.zeros_like(trow)
        put_totals(s, 0, tacc, trow)
        m = mask[...].astype(F32)
        trow[pl.ds(s[0] * 2 + s[2] + 8, 1), :] = (m[0:1, :] + m[1:2, :]) * (1.0 / NP)


def e2_body(s, w, b10, b11, trow1, send, trow, tacc, wv, si):
    ins = copier(lambda j: w.at[j], lambda j: wv.at[j], si)
    start_all(Z, ins)
    send[...] = jnp.zeros_like(send)
    tacc[...] = jnp.zeros_like(tacc)
    for j in range(Z):
        ins(j).wait()
        e_step(wv[j], (b10, b11), send, tacc)
    trow[...] = trow1[...]
    put_totals(s, 1, tacc, trow)
    send[2 * CR : 2 * CR + 16, :] = trow[...]


def put_rows(racc, rsc):
    for k in range(8):
        rsc[k : k + 1, :] = racc[0:1, k * 256 : (k + 1) * 256]


def k_body(s, w, za, zb, epoch, after, b00, b10, kt, rz, group, racc, rsc, so):
    i = pl.program_id(0)

    size = CR + TE
    outs = [
        pltpu.make_async_copy(blk, group.at[pl.ds(q * size, size), :], so.at[q])
        for q, blk in enumerate((b00, b10))
    ]

    @pl.when(i == 0)
    def _():
        for copy in outs:
            copy.start()
        racc[...] = jnp.zeros_like(racc)

    tau = 0.04 + 0.001 * epoch[0:1, 0:1].astype(F32)
    factor = LOG2E / tau
    wn, _ = unit(w[...])
    wb = wn.astype(BF16)
    half = NT // 2
    ka = jnp.exp2(dot(wb, za[...], 1, 1) * factor)
    kb = jnp.exp2(dot(wb, zb[...], 1, 1) * factor)
    kt[0, :, 0:half] = ka
    kt[0, :, half:NT] = kb
    c = 1.0 / (jnp.sum(ka, axis=1, keepdims=True) + jnp.sum(kb, axis=1, keepdims=True))
    racc[0:1, 0:half] += jnp.sum(ka * c, axis=0, keepdims=True)
    racc[0:1, half:NT] += jnp.sum(kb * c, axis=0, keepdims=True)

    @pl.when(i == pl.num_programs(0) - 1)
    def _():
        put_rows(racc, rsc)
        for b in range(Z):
            rz[b] = rsc[...]
        for copy in outs:
            copy.wait()


def mid1_body(s, rz, tpk, tin, after, out):
    r = jnp.sum(rz[...], axis=0)
    ab = tpk[...] + tin[2 * CR : 2 * CR + 16, :]
    for b in range(C * NP):
        out[b, 0:8, :] = r
        out[b, 8:12, :] = ab[0:4]
        out[b, 12:16, :] = ab[8:12]


def mid2_body(s, rz, keep, tin, out, g):
    c = s[2]
    r = jnp.sum(rz[:, 0:8, :], axis=0)
    g[...] = keep[...] + tin[0 : 2 * CR, :]
    for cd in range(C):
        for p in range(NP):
            out[cd * NP + p, 0:8, :] = r
            out[cd * NP + p, 8:40, :] = g[pl.ds((c ^ cd) * CR + p * 32, 32), :]


def row_total(s, got, sc):
    c = s[2]
    same = jnp.zeros((8, D), F32)
    other = jnp.zeros((8, D), F32)
    for p in range(NP):
        same = same + got[c * NP + p, 0:8, :]
        other = other + got[(1 - c) * NP + p, 0:8, :]
    sc[0:4, :] = same[0:4] + other[4:8]
    sc[4:8, :] = same[4:8] + other[0:4]


def scales(s, got, rsc, u):
    row_total(s, got, rsc)
    inv = 1.0 / rsc[...]
    for k in range(8):
        u[0:1, k * 256 : (k + 1) * 256] = inv[k : k + 1, :]


def it2_body(s, kt, got, rz, racc, rsc, u, a, kv, si):
    ins = copier(lambda k: kt.at[k], lambda k: kv.at[k], si)
    start_all(KC, ins)
    racc[...] = jnp.zeros_like(racc)
    scales(s, got, rsc, u)
    tot = jnp.sum(got[:, 8:16, :], axis=0)
    a[0:4, :] = tot[4:8] / tot[0:4]
    a[4:8, :] = tot[4:8]

    def step(j):
        ins(j).wait()
        k = kv[j]
        c = 1.0 / jnp.sum(k * u[...], axis=1, keepdims=True)
        racc[...] += jnp.sum(k * c, axis=0, keepdims=True)

    loop(KC, step)
    put_rows(racc, rsc)
    for b in range(Z):
        rz[b, 0:8, :] = rsc[...]
        rz[b, 8:16, :] = a[...]


def it3_body(s, kt, got, rz, ccol, racc, rsc, u, crow, kv, si):
    ins = copier(lambda k: kt.at[k], lambda k: kv.at[k], si)
    start_all(KC, ins)
    racc[...] = jnp.zeros_like(racc)
    crow[...] = jnp.zeros_like(crow)
    scales(s, got, rsc, u)

    def step(j):
        ins(j).wait()
        k = kv[j]
        ku = k * u[...]
        t = ku[:, 0:128]
        for a in range(1, NT // 128):
            t = t + ku[:, a * 128 : (a + 1) * 128]
        c = 1.0 / jnp.sum(t, axis=1, keepdims=True)
        ccol[j] = jnp.broadcast_to(c, (KR, 128))
        crow[pl.ds(j, 1), :] = 1.0 / jnp.sum(t.T, axis=0, keepdims=True)
        racc[...] += jnp.sum(k * c, axis=0, keepdims=True)

    loop(KC, step)
    put_rows(racc, rsc)
    for b in range(Z):
        rz[b, 0:8, :] = rsc[...]
        rz[b, 8:16, :] = crow[...]


def gw_body(s, w, h_own, h_other, rz, after, out, done, wb):
    yh, c = s[0], s[2]

    @pl.when(pl.program_id(0) == 0)
    def _():
        wn, _ = unit(w[...])
        wb[...] = wn.astype(BF16)
        out[...] = jnp.zeros_like(out)
        done[...] = jnp.zeros_like(done)

    for j in range(2):
        acc = None
        for q in range(4):
            zq = (h_own, h_other)[q % 2][j, (q // 2) * (CR + TE) : (q // 2) * (CR + TE) + CR, :]
            at = 8 + (yh ^ (q // 2)) * 2 + (c ^ (q % 2))
            a = rz[pl.program_id(0) * 2 + j, pl.ds(at, 1), :]
            e = jnp.exp2(dot(wb[...], zq, 1, 1) * (STUDENT * LOG2E)) * a
            part = dot(e.astype(BF16), zq)
            acc = part if acc is None else acc + part
        out[...] += acc


def cw_body(s, w, za, zb, epoch, rz, after, keep, send, zp, acc):
    i = pl.program_id(0)
    c = s[2]

    @pl.when(i == 0)
    def _():
        zp[0:TE, :] = za[...]
        zp[TE : 2 * TE, :] = zb[...]
        acc[...] = jnp.zeros_like(acc)

    factor = LOG2E / (0.04 + 0.001 * epoch[0:1, 0:1].astype(F32))
    part = None
    for j in range(CWS):
        wb = w[j]
        e = jnp.exp2(dot(zp[...], wb, 1, 1) * factor)
        at = i * CWS + j
        yy, zz = at // Z, at % Z
        for h in range(2):
            row = rz[zz, pl.ds(8 + 2 * yy + h, 1), :]
            codes = (e[:, h * 256 : (h + 1) * 256] * row).astype(BF16)
            one = dot(codes, wb[h * 256 : (h + 1) * 256])
            part = one if part is None else part + one
    acc[...] += part

    @pl.when(i == pl.num_programs(0) - 1)
    def _():
        r = jnp.sum(rz[:, 0:8, :], axis=0)
        keep[0:8, :] = r
        keep[8 : 8 + TE, :] = acc[0:TE, :]
        send[0:4, :] = r[4:8]
        send[4:8, :] = r[0:4]
        send[8 : 8 + TE, :] = acc[TE : 2 * TE, :]


def mid3_body(s, keep, tin, got2, out):
    pack = keep[...] + tin[...]
    g = jnp.sum(got2[:, 8:40, :], axis=0)
    for p in range(NP):
        out[p, 0:72, :] = pack
        out[p, 72:104, :] = g


def last_body(
    s, sf, pairs, mask, got1, got3, kt, ccol, h_own, h_other, gwp, w,
    loss, feats, protos,
    rsc, trow, g, hv, kv, cv, u_all, si,
):
    n = KC // YH
    ks = copier(lambda k: kt.at[s[0] * n + k], lambda k: kv.at[k], si)
    start_all(n, ks)

    def crops(h, cc):
        def copy(at):
            block = (at // Z) ^ s[0]
            to = cc * YH * Z + at
            return pltpu.make_async_copy(
                h.at[at % Z, pl.ds(block * (CR + TE) + CR, TE), :],
                hv.at[pl.ds(to * TE, TE), :],
                si.at[n + to],
            )

        return copy

    crops_own, crops_other = crops(h_own, 0), crops(h_other, 1)
    start_all(YH * Z, crops_own)
    start_all(YH * Z, crops_other)
    more = pltpu.make_async_copy(ccol.at[pl.ds(s[0] * n, n)], cv, si.at[n + 32])
    more.start()

    yh, z, c = s[0], s[1], s[2]
    zs, inv = unit(sf[...])
    zsb = zs.astype(BF16).astype(F32)
    trow[...] = jnp.sum(got1[:, 8:16, :], axis=0)
    at = yh * 2 + c
    t = trow[pl.ds(at, 1), :]
    msum = trow[pl.ds(at + 4, 1), :]
    a = jnp.broadcast_to(msum / t, (128, CR)).T[:, 0:1]
    rsc[...] = 1.0 / jnp.sum(got3[:, 0:8, :], axis=0)
    own = yh * Z + z
    row = rsc[pl.ds(own // 4, 1), :]
    u = row[:, 0:128]
    u = jnp.where(own % 4 >= 2, row[:, 128:256], u)
    col = jnp.broadcast_to(u, (128, 128)).T
    ucol = jnp.where(own % 2 == 1, col[TE : 2 * TE, 0:1], col[0:TE, 0:1])
    cw = jnp.sum(got3[:, 8:72, :], axis=0) * ucol
    for p in range(NP):
        g[p * 32 : (p + 1) * 32, :] = got3[p, 72:104, :]
    q = dot(selector(pairs, mask), cw, 0, 0, lax.Precision.HIGHEST)
    cross = dot(jnp.ones((8, D), F32), zsb * q, 1, 1, lax.Precision.HIGHEST)
    loss[...] = msum * jnp.log(t) - STUDENT * cross[0:1, :]
    gz = SCALE * (a * g[...] - q)
    feats[...] = (gz - zs * jnp.sum(zs * gz, axis=1, keepdims=True)) * inv

    for k in range(8):
        u_all[0:1, k * D : (k + 1) * D] = rsc[k : k + 1, :]
    wait_all(YH * Z, crops_own)
    wait_all(YH * Z, crops_other)
    more.wait()

    def step(k):
        ks(k).wait()
        acc = dot((kv[k] * u_all[...]).astype(BF16), hv[...])
        rows = pl.ds(k * KR, KR)
        wn, inv_w = unit(w[rows, :])
        gw = SCALE * (gwp[rows, :] - acc * cv[k, :, 0:1])
        protos[rows, :] = (gw - wn * jnp.sum(wn * gw, axis=1, keepdims=True)) * inv_w

    loop(n, step)


def local(student, teacher, prototypes, pairs, mask, epoch):
    yh, z, c = lax.axis_index("yh"), lax.axis_index("z"), lax.axis_index("c")
    p = lax.axis_index(("yl", "x"))
    idx = jnp.stack([yh, z, c, p]).astype(jnp.int32)
    ep = epoch.reshape(1, 1)
    student, teacher, protos = hbm(student), hbm(teacher), hbm(prototypes)
    pairs, mask = hbm(pairs.T), hbm(mask.T)
    chunked = hbm(prototypes.reshape(YH * Z, C, SH, D))
    swap = [(0, 1), (1, 0)]
    prc = ("c", "yl", "x")

    spay, trep = call(
        prep_body, idx, 1,
        (student, teacher, pairs, mask),
        [whole((CR, D)), whole((TE, D)), whole((2, CR)), whole((2, CR))],
        [sds((CR + TE, D), BF16), sds((YH * Z, TE, D), BF16)],
        [whole((CR + TE, D)), whole((YH * Z, TE, D))],
        nbytes=1 << 20,
    )
    b00 = spay
    b01 = lax.ppermute(b00, "c", swap)
    b10 = lax.ppermute(b00, "yh", swap)
    za = lax.all_to_all(trep, ("yh", "z"), 0, 0, tiled=True).reshape(NT // 2, D)
    wbuf = pltpu.VMEM((Z, SH, D), BF16)
    tbuf = pltpu.VMEM((2 * CR, 128), F32)
    half = Z // 2
    pair_spec = spec((2, SH, D), lambda i, s: (i, 0, 0))
    keep, trow1, wnb = call(
        e1_body, idx, half,
        (chunked, b00, b01, mask),
        [spec((2, 1, SH, D), lambda i, s: (s[0] * half + i, s[2], 0, 0))]
        + [whole((CR + TE, D))] * 2
        + [whole((2, CR))],
        [sds((2 * CR, D), F32), sds((16, D), F32), pltpu.HBM((Z, SH, D), BF16)],
        [whole((2 * CR, D)), whole((16, D)), pair_spec],
        [tbuf], flops=4 << 30, nbytes=4 << 20,
    )
    b10, trow1 = lax.optimization_barrier((b10, trow1))
    b11 = lax.ppermute(b10, "c", swap)
    send, tpk = call(
        e2_body, idx, 1,
        (hbm(wnb), b10, b11, trow1),
        [ANY] + [whole((CR + TE, D))] * 2 + [whole((16, D))],
        [sds((2 * CR + 16, D), F32), sds((16, D), F32)],
        [whole((2 * CR + 16, D)), whole((16, D))],
        [tbuf, wbuf, sems(Z)], flops=4 << 30, nbytes=4 << 20,
    )
    tin = lax.ppermute(send, "yh", swap)
    za, tpk = lax.optimization_barrier((za, tpk))
    zb = lax.ppermute(za, "c", swap)

    kbuf = pltpu.VMEM((KC, KR, NT), F32)
    kt_spec = spec((1, KR, NT), lambda i, s: (i, 0, 0))
    per = SH // KR
    kt, rz1, group = call(
        k_body, idx, KC,
        (protos, za, zb, ep, tpk, b00, b10),
        [
            spec((KR, D), lambda i, s: ((((i // per) * Z + s[1]) * C + s[2]) * per + i % per, 0)),
            whole((NT // 2, D)), whole((NT // 2, D)), whole((1, 1)), ANY, ANY, ANY,
        ],
        [
            pltpu.HBM((KC, KR, NT), F32), sds((Z, 8, D), F32),
            pltpu.HBM((2 * (CR + TE), D), BF16),
        ],
        [kt_spec, whole((Z, 8, D)), ANY],
        [pltpu.VMEM((1, NT), F32), pltpu.VMEM((8, D), F32), sems(2)],
        flops=4 << 30, nbytes=10 << 20,
    )
    h_own = lax.all_gather(group, "z", axis=0, tiled=False)
    wall = pltpu.VMEM((YH * Z, SH, D), BF16)
    wnc, done = call(
        norm_body, idx, 1,
        (chunked, rz1),
        [ANY, ANY],
        [pltpu.HBM((YH * Z, SH, D), BF16), sds((8, 128), F32)],
        [ANY, whole((8, 128))],
        [wall, wall, sems(YH * Z), sems(YH * Z)],
        flops=2 << 30, nbytes=8 << 20,
    )
    rz1 = lax.all_to_all(rz1, "z", 0, 0, tiled=True)
    pay1 = call(
        mid1_body, idx, 1,
        (rz1, tpk, tin, done),
        [whole((Z, 8, D)), whole((16, D)), whole((2 * CR + 16, D)), ANY],
        sds((C * NP, 16, D), F32), whole((C * NP, 16, D)),
        nbytes=1 << 19,
    )
    got1 = lax.all_to_all(pay1, prc, 0, 0, tiled=True)

    it_scratch = [pltpu.VMEM((1, NT), F32), pltpu.VMEM((8, D), F32), pltpu.VMEM((1, NT), F32)]
    rz2 = call(
        it2_body, idx, 1,
        (hbm(kt), got1),
        [ANY, whole((C * NP, 16, D))],
        sds((Z, 16, D), F32), whole((Z, 16, D)),
        it_scratch + [pltpu.VMEM((8, D), F32), kbuf, sems(KC)], nbytes=9 << 20,
    )
    rz2 = lax.all_to_all(rz2, "z", 0, 0, tiled=True)
    pay2 = call(
        mid2_body, idx, 1,
        (rz2, keep, tin),
        [whole((Z, 16, D)), whole((2 * CR, D)), whole((2 * CR + 16, D))],
        sds((C * NP, 40, D), F32), whole((C * NP, 40, D)),
        [pltpu.VMEM((2 * CR, D), F32)],
        nbytes=2 << 20,
    )
    got2 = lax.all_to_all(pay2, prc, 0, 0, tiled=True)
    h_own, got2 = lax.optimization_barrier((h_own, got2))
    h_other = lax.ppermute(h_own, "c", swap)
    rz3, ccol = call(
        it3_body, idx, 1,
        (hbm(kt), got2),
        [ANY, whole((C * NP, 40, D))],
        [sds((Z, 16, D), F32), pltpu.HBM((KC, KR, 128), F32)],
        [whole((Z, 16, D)), whole((KC, KR, 128))],
        it_scratch + [pltpu.VMEM((8, D), F32), kbuf, sems(KC)], nbytes=9 << 20,
    )
    gwp, done3 = call(
        gw_body, idx, half,
        (protos, hbm(h_own), hbm(h_other), rz2, rz3),
        [
            spec((SH, D), lambda i, s: ((s[0] * Z + s[1]) * C + s[2], 0)),
            spec((2, 2 * (CR + TE), D), lambda i, s: (i, 0, 0)),
            spec((2, 2 * (CR + TE), D), lambda i, s: (i, 0, 0)),
            whole((Z, 16, D)), ANY,
        ],
        [sds((SH, D), F32), sds((8, 128), F32)],
        [whole((SH, D)), whole((8, 128))],
        [pltpu.VMEM((SH, D), BF16)],
        flops=8 << 30, nbytes=8 << 20,
    )
    rz3 = lax.all_to_all(rz3, "z", 0, 0, tiled=True)
    keep3, send3 = call(
        cw_body, idx, YH * Z // CWS,
        (hbm(wnc), za, zb, ep, rz3, done3),
        [
            spec((CWS, SH, D), lambda i, s: (i, 0, 0)),
            spec((TE, D), lambda i, s: (s[0] * Z + s[1], 0)),
            spec((TE, D), lambda i, s: (s[0] * Z + s[1], 0)),
            whole((1, 1)), whole((Z, 16, D)), ANY,
        ],
        [sds((8 + TE, D), F32)] * 2, [whole((8 + TE, D))] * 2,
        [pltpu.VMEM((2 * TE, D), BF16), pltpu.VMEM((2 * TE, D), F32)],
        flops=1 << 30, nbytes=6 << 20,
    )
    tin3 = lax.ppermute(send3, "c", swap)
    pay3 = call(
        mid3_body, idx, 1,
        (keep3, tin3, got2),
        [whole((8 + TE, D))] * 2 + [whole((C * NP, 40, D))],
        sds((NP, 104, D), F32), whole((NP, 104, D)),
        nbytes=2 << 20,
    )
    got3 = lax.all_to_all(pay3, ("yl", "x"), 0, 0, tiled=True)

    n = KC // YH
    loss, grad_feats, grad_proto = call(
        last_body, idx, 1,
        (student, pairs, mask, got1, got3, hbm(kt), hbm(ccol), hbm(h_own), hbm(h_other), gwp, protos),
        [
            whole((CR, D)), whole((2, CR)), whole((2, CR)),
            whole((C * NP, 16, D)), whole((NP, 104, D)),
            ANY, ANY, ANY, ANY, whole((SH, D)),
            spec((SH, D), lambda i, s: ((s[0] * Z + s[1]) * C + s[2], 0)),
        ],
        [sds((1, CR), F32), sds((CR, D), F32), sds((SH, D), F32)],
        [whole((1, CR)), whole((CR, D)), whole((SH, D))],
        [
            pltpu.VMEM((8, D), F32), pltpu.VMEM((8, D), F32), pltpu.VMEM((CR, D), F32),
            pltpu.VMEM((NT, D), BF16), pltpu.VMEM((n, KR, NT), F32),
            pltpu.VMEM((n, KR, 128), F32), pltpu.VMEM((1, NT), F32), sems(n + 33),
        ],
        flops=1 << 30, nbytes=8 << 20,
    )
    return loss.reshape(CR), grad_feats, grad_proto


def solution(mesh):
    fine = Mesh(mesh.devices.reshape(YH, Z, C, YL, X), ("yh", "z", "c", "yl", "x"))
    dp, proto = ("yh", "z", "c"), ("yl", "x")
    in_specs = (P(dp, None), P(dp, None), P(proto, None), P(dp, None), P(dp, None), P())
    out_specs = (P(dp), P(dp, None), P(proto + dp, None))
    return jax.shard_map(local, mesh=fine, in_specs=in_specs, out_specs=out_specs, check_vma=False)
```

```python
import jax
import jax.numpy as jnp
from jax import lax
from jax.experimental import pallas as pl
from jax.experimental.pallas import tpu as pltpu
from jax.sharding import Mesh, PartitionSpec as P

F32, BF16 = jnp.float32, jnp.bfloat16
YH, Z, C, YL, X = 2, 8, 2, 2, 4
NP = YL * X
D = 256
CR = 256
TE = 64
NT = YH * Z * C * TE
SH = 512
EPS = 1e-6
LOG2E = 1.4426950408889634
STUDENT = 10.0
SCALE = 2560.0
MIB = 1 << 20
KC, KR = 4, 256
CWS = 8


def dot(a, b, ca=1, cb=0, precision=None):
    return lax.dot_general(
        a, b, (((ca,), (cb,)), ((), ())), preferred_element_type=F32, precision=precision
    )


def unit(values):
    wide = values.astype(F32)
    inv = lax.rsqrt(jnp.sum(wide * wide, axis=1, keepdims=True) + EPS)
    return wide * inv, inv


def params(mib):
    return pltpu.CompilerParams(vmem_limit_bytes=mib * MIB, dimension_semantics=("arbitrary",))


def hbm(x):
    return pltpu.with_memory_space_constraint(x, pltpu.HBM)


ANY = pl.BlockSpec(memory_space=pl.ANY)


def call(body, idx, grid, ins, in_specs, outs, out_specs, scratch=(), mib=24, flops=0, nbytes=0, alias={}):
    return pl.pallas_call(
        body,
        grid_spec=pltpu.PrefetchScalarGridSpec(
            num_scalar_prefetch=1,
            grid=(grid,),
            in_specs=in_specs,
            out_specs=out_specs,
            scratch_shapes=list(scratch),
        ),
        out_shape=outs,
        compiler_params=params(mib),
        input_output_aliases=alias,
        cost_estimate=pl.CostEstimate(flops=flops, bytes_accessed=nbytes, transcendentals=0),
    )(idx, *ins)


def loop(n, body):
    lax.fori_loop(0, n, lambda k, x: (body(k), x)[1], 0)


def copier(source, target, sem):
    return lambda k: pltpu.make_async_copy(source(k), target(k), sem.at[k])


def start_all(n, copy):
    loop(n, lambda k: copy(k).start())


def wait_all(n, copy):
    loop(n, lambda k: copy(k).wait())


def sems(n):
    return pltpu.SemaphoreType.DMA((n,))


def whole(shape):
    zeros = (0,) * len(shape)
    return pl.BlockSpec(shape, lambda i, s: zeros)


def spec(shape, fn):
    return pl.BlockSpec(shape, fn)


def sds(shape, dtype):
    return jax.ShapeDtypeStruct(shape, dtype)


def selector(pairs, mask):
    rows = lax.broadcasted_iota(jnp.int32, (TE, CR), 0)
    m = mask[...].astype(F32)
    return jnp.where(pairs[0:1, :] == rows, m[0:1, :], 0.0) + jnp.where(
        pairs[1:2, :] == rows, m[1:2, :], 0.0
    )


def prep_body(s, sf, tf, pairs, mask, spay, trep):
    zs, _ = unit(sf[...])
    zsb = zs.astype(BF16)
    spay[0:CR, :] = zsb
    spay[CR : CR + TE, :] = dot(selector(pairs, mask).astype(BF16), zsb).astype(BF16)
    zt, _ = unit(tf[...])
    ztb = zt.astype(BF16)
    for b in range(YH * Z):
        trep[b] = ztb


def norm_body(s, w, after, out, done, wv, nv, si, so):
    n = YH * Z
    ins = copier(lambda j: w.at[j, s[2]], lambda j: wv.at[j], si)
    outs = copier(lambda j: nv.at[j], lambda j: out.at[j], so)
    start_all(n, ins)

    def step(j):
        ins(j).wait()
        wn, _ = unit(wv[j])
        nv[j] = wn.astype(BF16)
        outs(j).start()

    loop(n, step)
    done[...] = jnp.zeros_like(done)
    wait_all(n, outs)


def e_step(wb, z_refs, g, tacc):
    for q in range(2):
        rows = slice(q * CR, (q + 1) * CR)
        e = jnp.exp2(dot(z_refs[q][0:CR, :], wb, 1, 1) * (STUDENT * LOG2E))
        t = e[:, 0:128]
        for k in range(1, SH // 128):
            t = t + e[:, k * 128 : (k + 1) * 128]
        tacc[rows, :] += t
        g[rows, :] += dot(e.astype(BF16), wb)


def put_totals(s, yy, tacc, trow):
    yh, c = s[0], s[2]
    for q in range(2):
        t = jnp.sum(tacc[q * CR : (q + 1) * CR, :].T, axis=0, keepdims=True)
        trow[pl.ds((yh ^ yy) * 2 + (c ^ q), 1), :] = t


def e1_body(s, w, b00, b01, mask, keep, trow, wnb, tacc):
    @pl.when(pl.program_id(0) == 0)
    def _():
        keep[...] = jnp.zeros_like(keep)
        tacc[...] = jnp.zeros_like(tacc)

    for j in range(2):
        wn, _ = unit(w[j, 0])
        wb = wn.astype(BF16)
        wnb[j] = wb
        e_step(wb, (b00, b01), keep, tacc)

    @pl.when(pl.program_id(0) == pl.num_programs(0) - 1)
    def _():
        trow[...] = jnp.zeros_like(trow)
        put_totals(s, 0, tacc, trow)
        m = mask[...].astype(F32)
        trow[pl.ds(s[0] * 2 + s[2] + 8, 1), :] = (m[0:1, :] + m[1:2, :]) * (1.0 / NP)


def e2_body(s, w, b10, b11, trow1, b00, send, trow, group, tacc, wv, si, so):
    ins = copier(lambda j: w.at[j], lambda j: wv.at[j], si)
    start_all(Z, ins)
    size = CR + TE
    outs = [
        pltpu.make_async_copy(blk, group.at[pl.ds(q * size, size), :], so.at[q])
        for q, blk in enumerate((b00, b10))
    ]
    for copy in outs:
        copy.start()
    send[...] = jnp.zeros_like(send)
    tacc[...] = jnp.zeros_like(tacc)
    for j in range(Z):
        ins(j).wait()
        e_step(wv[j], (b10, b11), send, tacc)
    trow[...] = trow1[...]
    put_totals(s, 1, tacc, trow)
    send[2 * CR : 2 * CR + 16, :] = trow[...]
    for copy in outs:
        copy.wait()


def put_rows(racc, rsc):
    for k in range(8):
        rsc[k : k + 1, :] = racc[0:1, k * 256 : (k + 1) * 256]


def k_body(s, w, za, zb, epoch, after, kt, rz, racc, rsc):
    i = pl.program_id(0)

    @pl.when(i == 0)
    def _():
        racc[...] = jnp.zeros_like(racc)

    tau = 0.04 + 0.001 * epoch[0:1, 0:1].astype(F32)
    factor = LOG2E / tau
    wn, _ = unit(w[...])
    wb = wn.astype(BF16)
    half = NT // 2
    ka = jnp.exp2(dot(wb, za[...], 1, 1) * factor)
    kb = jnp.exp2(dot(wb, zb[...], 1, 1) * factor)
    kt[0, :, 0:half] = ka.astype(BF16)
    kt[0, :, half:NT] = kb.astype(BF16)
    c = 1.0 / (jnp.sum(ka, axis=1, keepdims=True) + jnp.sum(kb, axis=1, keepdims=True))
    racc[0:1, 0:half] += jnp.sum(ka * c, axis=0, keepdims=True)
    racc[0:1, half:NT] += jnp.sum(kb * c, axis=0, keepdims=True)

    @pl.when(i == pl.num_programs(0) - 1)
    def _():
        put_rows(racc, rsc)
        for b in range(Z):
            rz[b] = rsc[...]


def mid1_body(s, rz, tpk, tin, after, out):
    r = jnp.sum(rz[...], axis=0)
    ab = tpk[...] + tin[2 * CR : 2 * CR + 16, :]
    for b in range(C * NP):
        out[b, 0:8, :] = r
        out[b, 8:12, :] = ab[0:4]
        out[b, 12:16, :] = ab[8:12]


def mid2_body(s, rz, keep, tin, out, g):
    c = s[2]
    r = jnp.sum(rz[:, 0:8, :], axis=0)
    g[...] = keep[...] + tin[0 : 2 * CR, :]
    for cd in range(C):
        for p in range(NP):
            out[cd * NP + p, 0:8, :] = r
            out[cd * NP + p, 8:40, :] = g[pl.ds((c ^ cd) * CR + p * 32, 32), :]


def row_total(s, got, sc):
    c = s[2]
    same = jnp.zeros((8, D), F32)
    other = jnp.zeros((8, D), F32)
    for p in range(NP):
        same = same + got[c * NP + p, 0:8, :]
        other = other + got[(1 - c) * NP + p, 0:8, :]
    sc[0:4, :] = same[0:4] + other[4:8]
    sc[4:8, :] = same[4:8] + other[0:4]


def scales(s, got, rsc, u):
    row_total(s, got, rsc)
    inv = 1.0 / rsc[...]
    for k in range(8):
        u[0:1, k * 256 : (k + 1) * 256] = inv[k : k + 1, :]


def it2_body(s, kt, got, rz, racc, rsc, u, a, kv, si):
    ins = copier(lambda k: kt.at[k], lambda k: kv.at[k], si)
    start_all(KC, ins)
    racc[...] = jnp.zeros_like(racc)
    scales(s, got, rsc, u)
    tot = jnp.sum(got[:, 8:16, :], axis=0)
    a[0:4, :] = tot[4:8] / tot[0:4]
    a[4:8, :] = tot[4:8]

    def step(j):
        ins(j).wait()
        k = kv[j].astype(F32)
        c = 1.0 / jnp.sum(k * u[...], axis=1, keepdims=True)
        racc[...] += jnp.sum(k * c, axis=0, keepdims=True)

    loop(KC, step)
    put_rows(racc, rsc)
    for b in range(Z):
        rz[b, 0:8, :] = rsc[...]
        rz[b, 8:16, :] = a[...]


def it3_body(s, kt, got, rz, ccol, racc, rsc, u, crow, kv, si):
    ins = copier(lambda k: kt.at[k], lambda k: kv.at[k], si)
    start_all(KC, ins)
    racc[...] = jnp.zeros_like(racc)
    crow[...] = jnp.zeros_like(crow)
    scales(s, got, rsc, u)

    def step(j):
        ins(j).wait()
        k = kv[j].astype(F32)
        ku = k * u[...]
        t = ku[:, 0:128]
        for a in range(1, NT // 128):
            t = t + ku[:, a * 128 : (a + 1) * 128]
        c = 1.0 / jnp.sum(t, axis=1, keepdims=True)
        ccol[j] = jnp.broadcast_to(c, (KR, 128))
        crow[pl.ds(j, 1), :] = 1.0 / jnp.sum(t.T, axis=0, keepdims=True)
        racc[...] += jnp.sum(k * c, axis=0, keepdims=True)

    loop(KC, step)
    put_rows(racc, rsc)
    for b in range(Z):
        rz[b, 0:8, :] = rsc[...]
        rz[b, 8:16, :] = crow[...]


def gw_body(s, w, h_own, h_other, rz, after, out, done, wb):
    yh, c = s[0], s[2]

    @pl.when(pl.program_id(0) == 0)
    def _():
        wn, _ = unit(w[...])
        wb[...] = wn.astype(BF16)
        out[...] = jnp.zeros_like(out)
        done[...] = jnp.zeros_like(done)

    for j in range(2):
        acc = None
        for q in range(4):
            zq = (h_own, h_other)[q % 2][j, (q // 2) * (CR + TE) : (q // 2) * (CR + TE) + CR, :]
            at = 8 + (yh ^ (q // 2)) * 2 + (c ^ (q % 2))
            a = rz[pl.program_id(0) * 2 + j, pl.ds(at, 1), :]
            e = jnp.exp2(dot(wb[...], zq, 1, 1) * (STUDENT * LOG2E)) * a
            part = dot(e.astype(BF16), zq)
            acc = part if acc is None else acc + part
        out[...] += acc


def cw_body(s, w, za, zb, epoch, rz, after, keep, send, zp, acc):
    i = pl.program_id(0)
    c = s[2]

    @pl.when(i == 0)
    def _():
        zp[0:TE, :] = za[...]
        zp[TE : 2 * TE, :] = zb[...]
        acc[...] = jnp.zeros_like(acc)

    factor = LOG2E / (0.04 + 0.001 * epoch[0:1, 0:1].astype(F32))
    part = None
    for j in range(CWS):
        wb = w[j]
        e = jnp.exp2(dot(zp[...], wb, 1, 1) * factor)
        at = i * CWS + j
        yy, zz = at // Z, at % Z
        for h in range(2):
            row = rz[zz, pl.ds(8 + 2 * yy + h, 1), :]
            codes = (e[:, h * 256 : (h + 1) * 256] * row).astype(BF16)
            one = dot(codes, wb[h * 256 : (h + 1) * 256])
            part = one if part is None else part + one
    acc[...] += part

    @pl.when(i == pl.num_programs(0) - 1)
    def _():
        r = jnp.sum(rz[:, 0:8, :], axis=0)
        keep[0:8, :] = r
        keep[8 : 8 + TE, :] = acc[0:TE, :]
        send[0:4, :] = r[4:8]
        send[4:8, :] = r[0:4]
        send[8 : 8 + TE, :] = acc[TE : 2 * TE, :]


def mid3_body(s, keep, tin, got2, out):
    pack = keep[...] + tin[...]
    g = jnp.sum(got2[:, 8:40, :], axis=0)
    for p in range(NP):
        out[p, 0:72, :] = pack
        out[p, 72:104, :] = g


def last_body(
    s, sf, pairs, mask, got1, got3, kt, ccol, h_own, h_other, gwp, w,
    loss, feats, protos,
    rsc, trow, g, hv, kv, cv, u_all, si,
):
    n = KC // YH
    ks = copier(lambda k: kt.at[s[0] * n + k], lambda k: kv.at[k], si)
    start_all(n, ks)

    def crops(h, cc):
        def copy(at):
            block = (at // Z) ^ s[0]
            to = cc * YH * Z + at
            return pltpu.make_async_copy(
                h.at[at % Z, pl.ds(block * (CR + TE) + CR, TE), :],
                hv.at[pl.ds(to * TE, TE), :],
                si.at[n + to],
            )

        return copy

    crops_own, crops_other = crops(h_own, 0), crops(h_other, 1)
    start_all(YH * Z, crops_own)
    start_all(YH * Z, crops_other)
    more = pltpu.make_async_copy(ccol.at[pl.ds(s[0] * n, n)], cv, si.at[n + 32])
    more.start()

    yh, z, c = s[0], s[1], s[2]
    zs, inv = unit(sf[...])
    zsb = zs.astype(BF16).astype(F32)
    trow[...] = jnp.sum(got1[:, 8:16, :], axis=0)
    at = yh * 2 + c
    t = trow[pl.ds(at, 1), :]
    msum = trow[pl.ds(at + 4, 1), :]
    a = jnp.broadcast_to(msum / t, (128, CR)).T[:, 0:1]
    rsc[...] = 1.0 / jnp.sum(got3[:, 0:8, :], axis=0)
    own = yh * Z + z
    row = rsc[pl.ds(own // 4, 1), :]
    u = row[:, 0:128]
    u = jnp.where(own % 4 >= 2, row[:, 128:256], u)
    col = jnp.broadcast_to(u, (128, 128)).T
    ucol = jnp.where(own % 2 == 1, col[TE : 2 * TE, 0:1], col[0:TE, 0:1])
    cw = jnp.sum(got3[:, 8:72, :], axis=0) * ucol
    for p in range(NP):
        g[p * 32 : (p + 1) * 32, :] = got3[p, 72:104, :]
    q = dot(selector(pairs, mask), cw, 0, 0, lax.Precision.HIGHEST)
    cross = dot(jnp.ones((8, D), F32), zsb * q, 1, 1, lax.Precision.HIGHEST)
    loss[...] = msum * jnp.log(t) - STUDENT * cross[0:1, :]
    gz = SCALE * (a * g[...] - q)
    feats[...] = (gz - zs * jnp.sum(zs * gz, axis=1, keepdims=True)) * inv

    for k in range(8):
        u_all[0:1, k * D : (k + 1) * D] = rsc[k : k + 1, :]
    wait_all(YH * Z, crops_own)
    wait_all(YH * Z, crops_other)
    more.wait()

    def step(k):
        ks(k).wait()
        acc = dot((kv[k].astype(F32) * u_all[...]).astype(BF16), hv[...])
        rows = pl.ds(k * KR, KR)
        wn, inv_w = unit(w[rows, :])
        gw = SCALE * (gwp[rows, :] - acc * cv[k, :, 0:1])
        protos[rows, :] = (gw - wn * jnp.sum(wn * gw, axis=1, keepdims=True)) * inv_w

    loop(n, step)


def local(student, teacher, prototypes, pairs, mask, epoch):
    yh, z, c = lax.axis_index("yh"), lax.axis_index("z"), lax.axis_index("c")
    p = lax.axis_index(("yl", "x"))
    idx = jnp.stack([yh, z, c, p]).astype(jnp.int32)
    ep = epoch.reshape(1, 1)
    student, teacher, protos = hbm(student), hbm(teacher), hbm(prototypes)
    pairs, mask = hbm(pairs.T), hbm(mask.T)
    chunked = hbm(prototypes.reshape(YH * Z, C, SH, D))
    swap = [(0, 1), (1, 0)]
    prc = ("c", "yl", "x")

    spay, trep = call(
        prep_body, idx, 1,
        (student, teacher, pairs, mask),
        [whole((CR, D)), whole((TE, D)), whole((2, CR)), whole((2, CR))],
        [sds((CR + TE, D), BF16), sds((YH * Z, TE, D), BF16)],
        [whole((CR + TE, D)), whole((YH * Z, TE, D))],
        nbytes=1 << 20,
    )
    b00 = spay
    b01 = lax.ppermute(b00, "c", swap)
    b10 = lax.ppermute(b00, "yh", swap)
    za = lax.all_to_all(trep, ("yh", "z"), 0, 0, tiled=True).reshape(NT // 2, D)
    wbuf = pltpu.VMEM((Z, SH, D), BF16)
    tbuf = pltpu.VMEM((2 * CR, 128), F32)
    half = Z // 2
    pair_spec = spec((2, SH, D), lambda i, s: (i, 0, 0))
    keep, trow1, wnb = call(
        e1_body, idx, half,
        (chunked, b00, b01, mask),
        [spec((2, 1, SH, D), lambda i, s: (s[0] * half + i, s[2], 0, 0))]
        + [whole((CR + TE, D))] * 2
        + [whole((2, CR))],
        [sds((2 * CR, D), F32), sds((16, D), F32), pltpu.HBM((Z, SH, D), BF16)],
        [whole((2 * CR, D)), whole((16, D)), pair_spec],
        [tbuf], flops=4 << 30, nbytes=4 << 20,
    )
    b10, trow1 = lax.optimization_barrier((b10, trow1))
    b11 = lax.ppermute(b10, "c", swap)
    send, tpk, group = call(
        e2_body, idx, 1,
        (hbm(wnb), b10, b11, trow1, b00),
        [ANY] + [whole((CR + TE, D))] * 2 + [whole((16, D)), ANY],
        [sds((2 * CR + 16, D), F32), sds((16, D), F32), pltpu.HBM((2 * (CR + TE), D), BF16)],
        [whole((2 * CR + 16, D)), whole((16, D)), ANY],
        [tbuf, wbuf, sems(Z), sems(2)], flops=4 << 30, nbytes=4 << 20,
    )
    tin = lax.ppermute(send, "yh", swap)
    za, tpk, group = lax.optimization_barrier((za, tpk, group))
    h_own = lax.all_gather(group, "z", axis=0, tiled=False)
    zb = lax.ppermute(za, "c", swap)

    kbuf = pltpu.VMEM((KC, KR, NT), BF16)
    kt_spec = spec((1, KR, NT), lambda i, s: (i, 0, 0))
    per = SH // KR
    kt, rz1 = call(
        k_body, idx, KC,
        (protos, za, zb, ep, tpk),
        [
            spec((KR, D), lambda i, s: ((((i // per) * Z + s[1]) * C + s[2]) * per + i % per, 0)),
            whole((NT // 2, D)), whole((NT // 2, D)), whole((1, 1)), ANY,
        ],
        [
            pltpu.HBM((KC, KR, NT), BF16), sds((Z, 8, D), F32),
        ],
        [kt_spec, whole((Z, 8, D))],
        [pltpu.VMEM((1, NT), F32), pltpu.VMEM((8, D), F32)],
        flops=4 << 30, nbytes=10 << 20,
    )
    wall = pltpu.VMEM((YH * Z, SH, D), BF16)
    wnc, done = call(
        norm_body, idx, 1,
        (chunked, rz1),
        [ANY, ANY],
        [pltpu.HBM((YH * Z, SH, D), BF16), sds((8, 128), F32)],
        [ANY, whole((8, 128))],
        [wall, wall, sems(YH * Z), sems(YH * Z)],
        flops=2 << 30, nbytes=8 << 20,
    )
    rz1 = lax.all_to_all(rz1, "z", 0, 0, tiled=True)
    pay1 = call(
        mid1_body, idx, 1,
        (rz1, tpk, tin, done),
        [whole((Z, 8, D)), whole((16, D)), whole((2 * CR + 16, D)), ANY],
        sds((C * NP, 16, D), F32), whole((C * NP, 16, D)),
        nbytes=1 << 19,
    )
    got1 = lax.all_to_all(pay1, prc, 0, 0, tiled=True)

    it_scratch = [pltpu.VMEM((1, NT), F32), pltpu.VMEM((8, D), F32), pltpu.VMEM((1, NT), F32)]
    rz2 = call(
        it2_body, idx, 1,
        (hbm(kt), got1),
        [ANY, whole((C * NP, 16, D))],
        sds((Z, 16, D), F32), whole((Z, 16, D)),
        it_scratch + [pltpu.VMEM((8, D), F32), kbuf, sems(KC)], nbytes=9 << 20,
    )
    rz2 = lax.all_to_all(rz2, "z", 0, 0, tiled=True)
    pay2 = call(
        mid2_body, idx, 1,
        (rz2, keep, tin),
        [whole((Z, 16, D)), whole((2 * CR, D)), whole((2 * CR + 16, D))],
        sds((C * NP, 40, D), F32), whole((C * NP, 40, D)),
        [pltpu.VMEM((2 * CR, D), F32)],
        nbytes=2 << 20,
    )
    got2 = lax.all_to_all(pay2, prc, 0, 0, tiled=True)
    h_own, got2 = lax.optimization_barrier((h_own, got2))
    h_other = lax.ppermute(h_own, "c", swap)
    rz3, ccol = call(
        it3_body, idx, 1,
        (hbm(kt), got2),
        [ANY, whole((C * NP, 40, D))],
        [sds((Z, 16, D), F32), pltpu.HBM((KC, KR, 128), F32)],
        [whole((Z, 16, D)), whole((KC, KR, 128))],
        it_scratch + [pltpu.VMEM((8, D), F32), kbuf, sems(KC)], nbytes=9 << 20,
    )
    gwp, done3 = call(
        gw_body, idx, half,
        (protos, hbm(h_own), hbm(h_other), rz2, rz3),
        [
            spec((SH, D), lambda i, s: ((s[0] * Z + s[1]) * C + s[2], 0)),
            spec((2, 2 * (CR + TE), D), lambda i, s: (i, 0, 0)),
            spec((2, 2 * (CR + TE), D), lambda i, s: (i, 0, 0)),
            whole((Z, 16, D)), ANY,
        ],
        [sds((SH, D), F32), sds((8, 128), F32)],
        [whole((SH, D)), whole((8, 128))],
        [pltpu.VMEM((SH, D), BF16)],
        flops=8 << 30, nbytes=8 << 20,
    )
    rz3 = lax.all_to_all(rz3, "z", 0, 0, tiled=True)
    keep3, send3 = call(
        cw_body, idx, YH * Z // CWS,
        (hbm(wnc), za, zb, ep, rz3, done3),
        [
            spec((CWS, SH, D), lambda i, s: (i, 0, 0)),
            spec((TE, D), lambda i, s: (s[0] * Z + s[1], 0)),
            spec((TE, D), lambda i, s: (s[0] * Z + s[1], 0)),
            whole((1, 1)), whole((Z, 16, D)), ANY,
        ],
        [sds((8 + TE, D), F32)] * 2, [whole((8 + TE, D))] * 2,
        [pltpu.VMEM((2 * TE, D), BF16), pltpu.VMEM((2 * TE, D), F32)],
        flops=1 << 30, nbytes=6 << 20,
    )
    tin3 = lax.ppermute(send3, "c", swap)
    pay3 = call(
        mid3_body, idx, 1,
        (keep3, tin3, got2),
        [whole((8 + TE, D))] * 2 + [whole((C * NP, 40, D))],
        sds((NP, 104, D), F32), whole((NP, 104, D)),
        nbytes=2 << 20,
    )
    got3 = lax.all_to_all(pay3, ("yl", "x"), 0, 0, tiled=True)

    n = KC // YH
    loss, grad_feats, grad_proto = call(
        last_body, idx, 1,
        (student, pairs, mask, got1, got3, hbm(kt), hbm(ccol), hbm(h_own), hbm(h_other), gwp, protos),
        [
            whole((CR, D)), whole((2, CR)), whole((2, CR)),
            whole((C * NP, 16, D)), whole((NP, 104, D)),
            ANY, ANY, ANY, ANY, whole((SH, D)),
            spec((SH, D), lambda i, s: ((s[0] * Z + s[1]) * C + s[2], 0)),
        ],
        [sds((1, CR), F32), sds((CR, D), F32), sds((SH, D), F32)],
        [whole((1, CR)), whole((CR, D)), whole((SH, D))],
        [
            pltpu.VMEM((8, D), F32), pltpu.VMEM((8, D), F32), pltpu.VMEM((CR, D), F32),
            pltpu.VMEM((NT, D), BF16), pltpu.VMEM((n, KR, NT), BF16),
            pltpu.VMEM((n, KR, 128), F32), pltpu.VMEM((1, NT), F32), sems(n + 33),
        ],
        flops=1 << 30, nbytes=8 << 20,
    )
    return loss.reshape(CR), grad_feats, grad_proto


def solution(mesh):
    fine = Mesh(mesh.devices.reshape(YH, Z, C, YL, X), ("yh", "z", "c", "yl", "x"))
    dp, proto = ("yh", "z", "c"), ("yl", "x")
    in_specs = (P(dp, None), P(dp, None), P(proto, None), P(dp, None), P(dp, None), P())
    out_specs = (P(dp), P(dp, None), P(proto + dp, None))
    return jax.shard_map(local, mesh=fine, in_specs=in_specs, out_specs=out_specs, check_vma=False)
```

```python
import jax
import jax.numpy as jnp
from jax import lax
from jax.experimental import pallas as pl
from jax.experimental.pallas import tpu as pltpu
from jax.sharding import Mesh, PartitionSpec as P

F32, BF16 = jnp.float32, jnp.bfloat16
YH, Z, C, YL, X = 2, 8, 2, 2, 4
NP = YL * X
D = 256
CR = 256
TE = 64
NT = YH * Z * C * TE
SH = 512
EPS = 1e-6
LOG2E = 1.4426950408889634
STUDENT = 10.0
SCALE = 2560.0
MIB = 1 << 20
KC, KR = 4, 256
CWS = 8


def dot(a, b, ca=1, cb=0, precision=None):
    return lax.dot_general(
        a, b, (((ca,), (cb,)), ((), ())), preferred_element_type=F32, precision=precision
    )


def unit(values):
    wide = values.astype(F32)
    inv = lax.rsqrt(jnp.sum(wide * wide, axis=1, keepdims=True) + EPS)
    return wide * inv, inv


def params(mib):
    return pltpu.CompilerParams(vmem_limit_bytes=mib * MIB, dimension_semantics=("arbitrary",))


def hbm(x):
    return pltpu.with_memory_space_constraint(x, pltpu.HBM)


ANY = pl.BlockSpec(memory_space=pl.ANY)


def call(body, idx, grid, ins, in_specs, outs, out_specs, scratch=(), mib=24, flops=0, nbytes=0, alias={}):
    return pl.pallas_call(
        body,
        grid_spec=pltpu.PrefetchScalarGridSpec(
            num_scalar_prefetch=1,
            grid=(grid,),
            in_specs=in_specs,
            out_specs=out_specs,
            scratch_shapes=list(scratch),
        ),
        out_shape=outs,
        compiler_params=params(mib),
        input_output_aliases=alias,
        cost_estimate=pl.CostEstimate(flops=flops, bytes_accessed=nbytes, transcendentals=0),
    )(idx, *ins)


def loop(n, body):
    lax.fori_loop(0, n, lambda k, x: (body(k), x)[1], 0)


def copier(source, target, sem):
    return lambda k: pltpu.make_async_copy(source(k), target(k), sem.at[k])


def start_all(n, copy):
    loop(n, lambda k: copy(k).start())


def wait_all(n, copy):
    loop(n, lambda k: copy(k).wait())


def sems(n):
    return pltpu.SemaphoreType.DMA((n,))


def whole(shape):
    zeros = (0,) * len(shape)
    return pl.BlockSpec(shape, lambda i, s: zeros)


def spec(shape, fn):
    return pl.BlockSpec(shape, fn)


def sds(shape, dtype):
    return jax.ShapeDtypeStruct(shape, dtype)


def selector(pairs, mask):
    rows = lax.broadcasted_iota(jnp.int32, (TE, CR), 0)
    m = mask[...].astype(F32)
    return jnp.where(pairs[0:1, :] == rows, m[0:1, :], 0.0) + jnp.where(
        pairs[1:2, :] == rows, m[1:2, :], 0.0
    )


def prep_body(s, sf, tf, pairs, mask, spay, trep):
    zs, _ = unit(sf[...])
    zsb = zs.astype(BF16)
    spay[0:CR, :] = zsb
    spay[CR : CR + TE, :] = dot(selector(pairs, mask).astype(BF16), zsb).astype(BF16)
    zt, _ = unit(tf[...])
    ztb = zt.astype(BF16)
    for b in range(YH * Z):
        trep[b] = ztb


def norm_body(s, w, after, out, done, wv, nv, si, so):
    n = YH * Z
    ins = copier(lambda j: w.at[j, s[2]], lambda j: wv.at[j], si)
    outs = copier(lambda j: nv.at[j], lambda j: out.at[j], so)
    start_all(n, ins)

    def step(j):
        ins(j).wait()
        wn, _ = unit(wv[j])
        nv[j] = wn.astype(BF16)
        outs(j).start()

    loop(n, step)
    done[...] = jnp.zeros_like(done)
    wait_all(n, outs)


def e_step(wb, z_refs, g, tacc):
    for q in range(2):
        rows = slice(q * CR, (q + 1) * CR)
        e = jnp.exp2(dot(z_refs[q][0:CR, :], wb, 1, 1) * (STUDENT * LOG2E))
        t = e[:, 0:128]
        for k in range(1, SH // 128):
            t = t + e[:, k * 128 : (k + 1) * 128]
        tacc[rows, :] += t
        g[rows, :] += dot(e.astype(BF16), wb)


def put_totals(s, yy, tacc, trow):
    yh, c = s[0], s[2]
    for q in range(2):
        t = jnp.sum(tacc[q * CR : (q + 1) * CR, :].T, axis=0, keepdims=True)
        trow[pl.ds((yh ^ yy) * 2 + (c ^ q), 1), :] = t


def e1_body(s, w, b00, b01, mask, keep, trow, wnb, tacc):
    @pl.when(pl.program_id(0) == 0)
    def _():
        keep[...] = jnp.zeros_like(keep)
        tacc[...] = jnp.zeros_like(tacc)

    for j in range(2):
        wn, _ = unit(w[j, 0])
        wb = wn.astype(BF16)
        wnb[j] = wb
        e_step(wb, (b00, b01), keep, tacc)

    @pl.when(pl.program_id(0) == pl.num_programs(0) - 1)
    def _():
        trow[...] = jnp.zeros_like(trow)
        put_totals(s, 0, tacc, trow)
        m = mask[...].astype(F32)
        trow[pl.ds(s[0] * 2 + s[2] + 8, 1), :] = (m[0:1, :] + m[1:2, :]) * (1.0 / NP)


def e2_body(s, w, b10, b11, trow1, b00, send, trow, group, tacc, wv, si, so):
    ins = copier(lambda j: w.at[j], lambda j: wv.at[j], si)
    start_all(Z, ins)
    size = CR + TE
    outs = [
        pltpu.make_async_copy(blk, group.at[pl.ds(q * size, size), :], so.at[q])
        for q, blk in enumerate((b00, b10))
    ]
    for copy in outs:
        copy.start()
    send[...] = jnp.zeros_like(send)
    tacc[...] = jnp.zeros_like(tacc)
    for j in range(Z):
        ins(j).wait()
        e_step(wv[j], (b10, b11), send, tacc)
    trow[...] = trow1[...]
    put_totals(s, 1, tacc, trow)
    send[2 * CR : 2 * CR + 16, :] = trow[...]
    for copy in outs:
        copy.wait()


def put_rows(racc, rsc):
    for k in range(8):
        rsc[k : k + 1, :] = racc[0:1, k * 256 : (k + 1) * 256]


def k_body(s, w, za, zb, epoch, after, kt, rz, racc, rsc):
    i = pl.program_id(0)

    @pl.when(i == 0)
    def _():
        racc[...] = jnp.zeros_like(racc)

    tau = 0.04 + 0.001 * epoch[0:1, 0:1].astype(F32)
    factor = LOG2E / tau
    wn, _ = unit(w[...])
    wb = wn.astype(BF16)
    half = NT // 2
    ka = jnp.exp2(dot(wb, za[...], 1, 1) * factor)
    kb = jnp.exp2(dot(wb, zb[...], 1, 1) * factor)
    kt[0, :, 0:half] = ka.astype(BF16)
    kt[0, :, half:NT] = kb.astype(BF16)
    c = 1.0 / (jnp.sum(ka, axis=1, keepdims=True) + jnp.sum(kb, axis=1, keepdims=True))
    racc[0:1, 0:half] += jnp.sum(ka * c, axis=0, keepdims=True)
    racc[0:1, half:NT] += jnp.sum(kb * c, axis=0, keepdims=True)

    @pl.when(i == pl.num_programs(0) - 1)
    def _():
        put_rows(racc, rsc)
        for b in range(Z):
            rz[b] = rsc[...]


def mid1_body(s, rz, tpk, tin, after, out):
    r = jnp.sum(rz[...], axis=0)
    ab = tpk[...] + tin[2 * CR : 2 * CR + 16, :]
    for b in range(C * NP):
        out[b, 0:8, :] = r
        out[b, 8:12, :] = ab[0:4]
        out[b, 12:16, :] = ab[8:12]


def mid2_body(s, rz, keep, tin, out, g):
    c = s[2]
    r = jnp.sum(rz[:, 0:8, :], axis=0)
    g[...] = keep[...] + tin[0 : 2 * CR, :]
    for cd in range(C):
        for p in range(NP):
            out[cd * NP + p, 0:8, :] = r
            out[cd * NP + p, 8:40, :] = g[pl.ds((c ^ cd) * CR + p * 32, 32), :]


def row_total(s, got, sc):
    c = s[2]
    same = jnp.zeros((8, D), F32)
    other = jnp.zeros((8, D), F32)
    for p in range(NP):
        same = same + got[c * NP + p, 0:8, :]
        other = other + got[(1 - c) * NP + p, 0:8, :]
    sc[0:4, :] = same[0:4] + other[4:8]
    sc[4:8, :] = same[4:8] + other[0:4]


def scales(s, got, rsc, u):
    row_total(s, got, rsc)
    inv = 1.0 / rsc[...]
    for k in range(8):
        u[0:1, k * 256 : (k + 1) * 256] = inv[k : k + 1, :]


def it2_body(s, kt, got, rz, racc, rsc, u, a, kv, si):
    ins = copier(lambda k: kt.at[k], lambda k: kv.at[k], si)
    start_all(KC, ins)
    racc[...] = jnp.zeros_like(racc)
    scales(s, got, rsc, u)
    tot = jnp.sum(got[:, 8:16, :], axis=0)
    a[0:4, :] = tot[4:8] / tot[0:4]
    a[4:8, :] = tot[4:8]

    def step(j):
        ins(j).wait()
        k = kv[j].astype(F32)
        c = 1.0 / jnp.sum(k * u[...], axis=1, keepdims=True)
        racc[...] += jnp.sum(k * c, axis=0, keepdims=True)

    loop(KC, step)
    put_rows(racc, rsc)
    for b in range(Z):
        rz[b, 0:8, :] = rsc[...]
        rz[b, 8:16, :] = a[...]


def it3_body(s, kt, got, rz, ccol, racc, rsc, u, crow, kv, si):
    ins = copier(lambda k: kt.at[k], lambda k: kv.at[k], si)
    start_all(KC, ins)
    racc[...] = jnp.zeros_like(racc)
    crow[...] = jnp.zeros_like(crow)
    scales(s, got, rsc, u)

    def step(j):
        ins(j).wait()
        k = kv[j].astype(F32)
        ku = k * u[...]
        t = ku[:, 0:128]
        for a in range(1, NT // 128):
            t = t + ku[:, a * 128 : (a + 1) * 128]
        c = 1.0 / jnp.sum(t, axis=1, keepdims=True)
        ccol[j] = jnp.broadcast_to(c, (KR, 128))
        crow[pl.ds(j, 1), :] = 1.0 / jnp.sum(t.T, axis=0, keepdims=True)
        racc[...] += jnp.sum(k * c, axis=0, keepdims=True)

    loop(KC, step)
    put_rows(racc, rsc)
    for b in range(Z):
        rz[b, 0:8, :] = rsc[...]
        rz[b, 8:16, :] = crow[...]


def gw_body(s, w, h_own, h_other, rz, after, out, done, wb):
    yh, c = s[0], s[2]

    @pl.when(pl.program_id(0) == 0)
    def _():
        wn, _ = unit(w[...])
        wb[...] = wn.astype(BF16)
        out[...] = jnp.zeros_like(out)
        done[...] = jnp.zeros_like(done)

    for j in range(2):
        acc = None
        for q in range(4):
            zq = (h_own, h_other)[q % 2][j, (q // 2) * (CR + TE) : (q // 2) * (CR + TE) + CR, :]
            at = 8 + (yh ^ (q // 2)) * 2 + (c ^ (q % 2))
            a = rz[pl.program_id(0) * 2 + j, pl.ds(at, 1), :]
            e = jnp.exp2(dot(wb[...], zq, 1, 1) * (STUDENT * LOG2E)) * a
            part = dot(e.astype(BF16), zq)
            acc = part if acc is None else acc + part
        out[...] += acc


def cw_body(s, w, za, zb, epoch, rz, after, keep, send, zp, acc):
    i = pl.program_id(0)
    c = s[2]

    @pl.when(i == 0)
    def _():
        zp[0:TE, :] = za[...]
        zp[TE : 2 * TE, :] = zb[...]
        acc[...] = jnp.zeros_like(acc)

    factor = LOG2E / (0.04 + 0.001 * epoch[0:1, 0:1].astype(F32))
    part = None
    for j in range(CWS):
        wb = w[j]
        e = jnp.exp2(dot(zp[...], wb, 1, 1) * factor).astype(BF16).astype(F32)
        at = i * CWS + j
        yy, zz = at // Z, at % Z
        for h in range(2):
            row = rz[zz, pl.ds(8 + 2 * yy + h, 1), :]
            codes = (e[:, h * 256 : (h + 1) * 256] * row).astype(BF16)
            one = dot(codes, wb[h * 256 : (h + 1) * 256])
            part = one if part is None else part + one
    acc[...] += part

    @pl.when(i == pl.num_programs(0) - 1)
    def _():
        r = jnp.sum(rz[:, 0:8, :], axis=0)
        keep[0:8, :] = r
        keep[8 : 8 + TE, :] = acc[0:TE, :]
        send[0:4, :] = r[4:8]
        send[4:8, :] = r[0:4]
        send[8 : 8 + TE, :] = acc[TE : 2 * TE, :]


def mid3_body(s, keep, tin, got2, out):
    pack = keep[...] + tin[...]
    g = jnp.sum(got2[:, 8:40, :], axis=0)
    for p in range(NP):
        out[p, 0:72, :] = pack
        out[p, 72:104, :] = g


def last_body(
    s, sf, pairs, mask, got1, got3, kt, ccol, h_own, h_other, gwp, w,
    loss, feats, protos,
    rsc, trow, g, hv, kv, cv, u_all, si,
):
    n = KC // YH
    ks = copier(lambda k: kt.at[s[0] * n + k], lambda k: kv.at[k], si)
    start_all(n, ks)

    def crops(h, cc):
        def copy(at):
            block = (at // Z) ^ s[0]
            to = cc * YH * Z + at
            return pltpu.make_async_copy(
                h.at[at % Z, pl.ds(block * (CR + TE) + CR, TE), :],
                hv.at[pl.ds(to * TE, TE), :],
                si.at[n + to],
            )

        return copy

    crops_own, crops_other = crops(h_own, 0), crops(h_other, 1)
    start_all(YH * Z, crops_own)
    start_all(YH * Z, crops_other)
    more = pltpu.make_async_copy(ccol.at[pl.ds(s[0] * n, n)], cv, si.at[n + 32])
    more.start()

    yh, z, c = s[0], s[1], s[2]
    zs, inv = unit(sf[...])
    zsb = zs.astype(BF16).astype(F32)
    trow[...] = jnp.sum(got1[:, 8:16, :], axis=0)
    at = yh * 2 + c
    t = trow[pl.ds(at, 1), :]
    msum = trow[pl.ds(at + 4, 1), :]
    a = jnp.broadcast_to(msum / t, (128, CR)).T[:, 0:1]
    rsc[...] = 1.0 / jnp.sum(got3[:, 0:8, :], axis=0)
    own = yh * Z + z
    row = rsc[pl.ds(own // 4, 1), :]
    u = row[:, 0:128]
    u = jnp.where(own % 4 >= 2, row[:, 128:256], u)
    col = jnp.broadcast_to(u, (128, 128)).T
    ucol = jnp.where(own % 2 == 1, col[TE : 2 * TE, 0:1], col[0:TE, 0:1])
    cw = jnp.sum(got3[:, 8:72, :], axis=0) * ucol
    for p in range(NP):
        g[p * 32 : (p + 1) * 32, :] = got3[p, 72:104, :]
    q = dot(selector(pairs, mask), cw, 0, 0, lax.Precision.HIGHEST)
    cross = dot(jnp.ones((8, D), F32), zsb * q, 1, 1, lax.Precision.HIGHEST)
    loss[...] = msum * jnp.log(t) - STUDENT * cross[0:1, :]
    gz = SCALE * (a * g[...] - q)
    feats[...] = (gz - zs * jnp.sum(zs * gz, axis=1, keepdims=True)) * inv

    for k in range(8):
        u_all[0:1, k * D : (k + 1) * D] = rsc[k : k + 1, :]
    wait_all(YH * Z, crops_own)
    wait_all(YH * Z, crops_other)
    more.wait()

    def step(k):
        ks(k).wait()
        acc = dot((kv[k].astype(F32) * u_all[...]).astype(BF16), hv[...])
        rows = pl.ds(k * KR, KR)
        wn, inv_w = unit(w[rows, :])
        gw = SCALE * (gwp[rows, :] - acc * cv[k, :, 0:1])
        protos[rows, :] = (gw - wn * jnp.sum(wn * gw, axis=1, keepdims=True)) * inv_w

    loop(n, step)


def local(student, teacher, prototypes, pairs, mask, epoch):
    yh, z, c = lax.axis_index("yh"), lax.axis_index("z"), lax.axis_index("c")
    p = lax.axis_index(("yl", "x"))
    idx = jnp.stack([yh, z, c, p]).astype(jnp.int32)
    ep = epoch.reshape(1, 1)
    student, teacher, protos = hbm(student), hbm(teacher), hbm(prototypes)
    pairs, mask = hbm(pairs.T), hbm(mask.T)
    chunked = hbm(prototypes.reshape(YH * Z, C, SH, D))
    swap = [(0, 1), (1, 0)]
    prc = ("c", "yl", "x")

    spay, trep = call(
        prep_body, idx, 1,
        (student, teacher, pairs, mask),
        [whole((CR, D)), whole((TE, D)), whole((2, CR)), whole((2, CR))],
        [sds((CR + TE, D), BF16), sds((YH * Z, TE, D), BF16)],
        [whole((CR + TE, D)), whole((YH * Z, TE, D))],
        nbytes=1 << 20,
    )
    b00 = spay
    b01 = lax.ppermute(b00, "c", swap)
    b10 = lax.ppermute(b00, "yh", swap)
    za = lax.all_to_all(trep, ("yh", "z"), 0, 0, tiled=True).reshape(NT // 2, D)
    wbuf = pltpu.VMEM((Z, SH, D), BF16)
    tbuf = pltpu.VMEM((2 * CR, 128), F32)
    half = Z // 2
    pair_spec = spec((2, SH, D), lambda i, s: (i, 0, 0))
    keep, trow1, wnb = call(
        e1_body, idx, half,
        (chunked, b00, b01, mask),
        [spec((2, 1, SH, D), lambda i, s: (s[0] * half + i, s[2], 0, 0))]
        + [whole((CR + TE, D))] * 2
        + [whole((2, CR))],
        [sds((2 * CR, D), F32), sds((16, D), F32), pltpu.HBM((Z, SH, D), BF16)],
        [whole((2 * CR, D)), whole((16, D)), pair_spec],
        [tbuf], flops=4 << 30, nbytes=4 << 20,
    )
    b10, trow1 = lax.optimization_barrier((b10, trow1))
    b11 = lax.ppermute(b10, "c", swap)
    send, tpk, group = call(
        e2_body, idx, 1,
        (hbm(wnb), b10, b11, trow1, b00),
        [ANY] + [whole((CR + TE, D))] * 2 + [whole((16, D)), ANY],
        [sds((2 * CR + 16, D), F32), sds((16, D), F32), pltpu.HBM((2 * (CR + TE), D), BF16)],
        [whole((2 * CR + 16, D)), whole((16, D)), ANY],
        [tbuf, wbuf, sems(Z), sems(2)], flops=4 << 30, nbytes=4 << 20,
    )
    tin = lax.ppermute(send, "yh", swap)
    za, tpk, group = lax.optimization_barrier((za, tpk, group))
    h_own = lax.all_gather(group, "z", axis=0, tiled=False)
    zb = lax.ppermute(za, "c", swap)

    kbuf = pltpu.VMEM((KC, KR, NT), BF16)
    kt_spec = spec((1, KR, NT), lambda i, s: (i, 0, 0))
    per = SH // KR
    kt, rz1 = call(
        k_body, idx, KC,
        (protos, za, zb, ep, tpk),
        [
            spec((KR, D), lambda i, s: ((((i // per) * Z + s[1]) * C + s[2]) * per + i % per, 0)),
            whole((NT // 2, D)), whole((NT // 2, D)), whole((1, 1)), ANY,
        ],
        [
            pltpu.HBM((KC, KR, NT), BF16), sds((Z, 8, D), F32),
        ],
        [kt_spec, whole((Z, 8, D))],
        [pltpu.VMEM((1, NT), F32), pltpu.VMEM((8, D), F32)],
        flops=4 << 30, nbytes=10 << 20,
    )
    wall = pltpu.VMEM((YH * Z, SH, D), BF16)
    wnc, done = call(
        norm_body, idx, 1,
        (chunked, rz1),
        [ANY, ANY],
        [pltpu.HBM((YH * Z, SH, D), BF16), sds((8, 128), F32)],
        [ANY, whole((8, 128))],
        [wall, wall, sems(YH * Z), sems(YH * Z)],
        flops=2 << 30, nbytes=8 << 20,
    )
    rz1 = lax.all_to_all(rz1, "z", 0, 0, tiled=True)
    pay1 = call(
        mid1_body, idx, 1,
        (rz1, tpk, tin, done),
        [whole((Z, 8, D)), whole((16, D)), whole((2 * CR + 16, D)), ANY],
        sds((C * NP, 16, D), F32), whole((C * NP, 16, D)),
        nbytes=1 << 19,
    )
    got1 = lax.all_to_all(pay1, prc, 0, 0, tiled=True)

    it_scratch = [pltpu.VMEM((1, NT), F32), pltpu.VMEM((8, D), F32), pltpu.VMEM((1, NT), F32)]
    rz2 = call(
        it2_body, idx, 1,
        (hbm(kt), got1),
        [ANY, whole((C * NP, 16, D))],
        sds((Z, 16, D), F32), whole((Z, 16, D)),
        it_scratch + [pltpu.VMEM((8, D), F32), kbuf, sems(KC)], nbytes=9 << 20,
    )
    rz2 = lax.all_to_all(rz2, "z", 0, 0, tiled=True)
    pay2 = call(
        mid2_body, idx, 1,
        (rz2, keep, tin),
        [whole((Z, 16, D)), whole((2 * CR, D)), whole((2 * CR + 16, D))],
        sds((C * NP, 40, D), F32), whole((C * NP, 40, D)),
        [pltpu.VMEM((2 * CR, D), F32)],
        nbytes=2 << 20,
    )
    got2 = lax.all_to_all(pay2, prc, 0, 0, tiled=True)
    h_own, got2 = lax.optimization_barrier((h_own, got2))
    h_other = lax.ppermute(h_own, "c", swap)
    rz3, ccol = call(
        it3_body, idx, 1,
        (hbm(kt), got2),
        [ANY, whole((C * NP, 40, D))],
        [sds((Z, 16, D), F32), pltpu.HBM((KC, KR, 128), F32)],
        [whole((Z, 16, D)), whole((KC, KR, 128))],
        it_scratch + [pltpu.VMEM((8, D), F32), kbuf, sems(KC)], nbytes=9 << 20,
    )
    gwp, done3 = call(
        gw_body, idx, half,
        (protos, hbm(h_own), hbm(h_other), rz2, rz3),
        [
            spec((SH, D), lambda i, s: ((s[0] * Z + s[1]) * C + s[2], 0)),
            spec((2, 2 * (CR + TE), D), lambda i, s: (i, 0, 0)),
            spec((2, 2 * (CR + TE), D), lambda i, s: (i, 0, 0)),
            whole((Z, 16, D)), ANY,
        ],
        [sds((SH, D), F32), sds((8, 128), F32)],
        [whole((SH, D)), whole((8, 128))],
        [pltpu.VMEM((SH, D), BF16)],
        flops=8 << 30, nbytes=8 << 20,
    )
    rz3 = lax.all_to_all(rz3, "z", 0, 0, tiled=True)
    keep3, send3 = call(
        cw_body, idx, YH * Z // CWS,
        (hbm(wnc), za, zb, ep, rz3, done3),
        [
            spec((CWS, SH, D), lambda i, s: (i, 0, 0)),
            spec((TE, D), lambda i, s: (s[0] * Z + s[1], 0)),
            spec((TE, D), lambda i, s: (s[0] * Z + s[1], 0)),
            whole((1, 1)), whole((Z, 16, D)), ANY,
        ],
        [sds((8 + TE, D), F32)] * 2, [whole((8 + TE, D))] * 2,
        [pltpu.VMEM((2 * TE, D), BF16), pltpu.VMEM((2 * TE, D), F32)],
        flops=1 << 30, nbytes=6 << 20,
    )
    tin3 = lax.ppermute(send3, "c", swap)
    pay3 = call(
        mid3_body, idx, 1,
        (keep3, tin3, got2),
        [whole((8 + TE, D))] * 2 + [whole((C * NP, 40, D))],
        sds((NP, 104, D), F32), whole((NP, 104, D)),
        nbytes=2 << 20,
    )
    got3 = lax.all_to_all(pay3, ("yl", "x"), 0, 0, tiled=True)

    n = KC // YH
    loss, grad_feats, grad_proto = call(
        last_body, idx, 1,
        (student, pairs, mask, got1, got3, hbm(kt), hbm(ccol), hbm(h_own), hbm(h_other), gwp, protos),
        [
            whole((CR, D)), whole((2, CR)), whole((2, CR)),
            whole((C * NP, 16, D)), whole((NP, 104, D)),
            ANY, ANY, ANY, ANY, whole((SH, D)),
            spec((SH, D), lambda i, s: ((s[0] * Z + s[1]) * C + s[2], 0)),
        ],
        [sds((1, CR), F32), sds((CR, D), F32), sds((SH, D), F32)],
        [whole((1, CR)), whole((CR, D)), whole((SH, D))],
        [
            pltpu.VMEM((8, D), F32), pltpu.VMEM((8, D), F32), pltpu.VMEM((CR, D), F32),
            pltpu.VMEM((NT, D), BF16), pltpu.VMEM((n, KR, NT), BF16),
            pltpu.VMEM((n, KR, 128), F32), pltpu.VMEM((1, NT), F32), sems(n + 33),
        ],
        flops=1 << 30, nbytes=8 << 20,
    )
    return loss.reshape(CR), grad_feats, grad_proto


def solution(mesh):
    fine = Mesh(mesh.devices.reshape(YH, Z, C, YL, X), ("yh", "z", "c", "yl", "x"))
    dp, proto = ("yh", "z", "c"), ("yl", "x")
    in_specs = (P(dp, None), P(dp, None), P(proto, None), P(dp, None), P(dp, None), P())
    out_specs = (P(dp), P(dp, None), P(proto + dp, None))
    return jax.shard_map(local, mesh=fine, in_specs=in_specs, out_specs=out_specs, check_vma=False)
```

```python
import jax
import jax.numpy as jnp
from jax import lax
from jax.experimental import pallas as pl
from jax.experimental.pallas import tpu as pltpu
from jax.sharding import Mesh, PartitionSpec as P

F32, BF16 = jnp.float32, jnp.bfloat16
YH, Z, C, YL, X = 2, 8, 2, 2, 4
NP = YL * X
D = 256
CR = 256
TE = 64
NT = YH * Z * C * TE
SH = 512
EPS = 1e-6
LOG2E = 1.4426950408889634
STUDENT = 10.0
SCALE = 2560.0
MIB = 1 << 20
KC, KR = 4, 256
CWS = 8


def dot(a, b, ca=1, cb=0, precision=None):
    return lax.dot_general(
        a, b, (((ca,), (cb,)), ((), ())), preferred_element_type=F32, precision=precision
    )


def unit(values):
    wide = values.astype(F32)
    inv = lax.rsqrt(jnp.sum(wide * wide, axis=1, keepdims=True) + EPS)
    return wide * inv, inv


def params(mib):
    return pltpu.CompilerParams(vmem_limit_bytes=mib * MIB, dimension_semantics=("arbitrary",))


def hbm(x):
    return pltpu.with_memory_space_constraint(x, pltpu.HBM)


ANY = pl.BlockSpec(memory_space=pl.ANY)


def call(body, idx, grid, ins, in_specs, outs, out_specs, scratch=(), mib=24, flops=0, nbytes=0, alias={}):
    return pl.pallas_call(
        body,
        grid_spec=pltpu.PrefetchScalarGridSpec(
            num_scalar_prefetch=1,
            grid=(grid,),
            in_specs=in_specs,
            out_specs=out_specs,
            scratch_shapes=list(scratch),
        ),
        out_shape=outs,
        compiler_params=params(mib),
        input_output_aliases=alias,
        cost_estimate=pl.CostEstimate(flops=flops, bytes_accessed=nbytes, transcendentals=0),
    )(idx, *ins)


def loop(n, body):
    lax.fori_loop(0, n, lambda k, x: (body(k), x)[1], 0)


def copier(source, target, sem):
    return lambda k: pltpu.make_async_copy(source(k), target(k), sem.at[k])


def start_all(n, copy):
    loop(n, lambda k: copy(k).start())


def wait_all(n, copy):
    loop(n, lambda k: copy(k).wait())


def sems(n):
    return pltpu.SemaphoreType.DMA((n,))


def whole(shape):
    zeros = (0,) * len(shape)
    return pl.BlockSpec(shape, lambda i, s: zeros)


def spec(shape, fn):
    return pl.BlockSpec(shape, fn)


def sds(shape, dtype):
    return jax.ShapeDtypeStruct(shape, dtype)


def selector(pairs, mask):
    rows = lax.broadcasted_iota(jnp.int32, (TE, CR), 0)
    m = mask[...].astype(F32)
    return jnp.where(pairs[0:1, :] == rows, m[0:1, :], 0.0) + jnp.where(
        pairs[1:2, :] == rows, m[1:2, :], 0.0
    )


def prep_body(s, sf, tf, pairs, mask, spay, trep):
    zs, _ = unit(sf[...])
    zsb = zs.astype(BF16)
    spay[0:CR, :] = zsb
    spay[CR : CR + TE, :] = dot(selector(pairs, mask).astype(BF16), zsb).astype(BF16)
    zt, _ = unit(tf[...])
    ztb = zt.astype(BF16)
    for b in range(YH * Z):
        trep[b] = ztb


def norm_body(s, w, after, out, done, wv, nv, si, so):
    n = YH * Z
    ins = copier(lambda j: w.at[j, s[2]], lambda j: wv.at[j], si)
    outs = copier(lambda j: nv.at[j], lambda j: out.at[j], so)
    start_all(n, ins)

    def step(j):
        ins(j).wait()
        wn, _ = unit(wv[j])
        nv[j] = wn.astype(BF16)
        outs(j).start()

    loop(n, step)
    done[...] = jnp.zeros_like(done)
    wait_all(n, outs)


def e_step(wb, z_refs, g, tacc):
    for q in range(2):
        rows = slice(q * CR, (q + 1) * CR)
        e = jnp.exp2(dot(z_refs[q][0:CR, :], wb, 1, 1) * (STUDENT * LOG2E))
        t = e[:, 0:128]
        for k in range(1, SH // 128):
            t = t + e[:, k * 128 : (k + 1) * 128]
        tacc[rows, :] += t
        g[rows, :] += dot(e.astype(BF16), wb)


def put_totals(s, yy, tacc, trow):
    yh, c = s[0], s[2]
    for q in range(2):
        t = jnp.sum(tacc[q * CR : (q + 1) * CR, :].T, axis=0, keepdims=True)
        trow[pl.ds((yh ^ yy) * 2 + (c ^ q), 1), :] = t


def e1_body(s, w, b00, b01, mask, keep, trow, wnb, tacc):
    @pl.when(pl.program_id(0) == 0)
    def _():
        keep[...] = jnp.zeros_like(keep)
        tacc[...] = jnp.zeros_like(tacc)

    for j in range(2):
        wn, _ = unit(w[j, 0])
        wb = wn.astype(BF16)
        wnb[j] = wb
        e_step(wb, (b00, b01), keep, tacc)

    @pl.when(pl.program_id(0) == pl.num_programs(0) - 1)
    def _():
        trow[...] = jnp.zeros_like(trow)
        put_totals(s, 0, tacc, trow)
        m = mask[...].astype(F32)
        trow[pl.ds(s[0] * 2 + s[2] + 8, 1), :] = (m[0:1, :] + m[1:2, :]) * (1.0 / NP)


def e2_body(s, w, b10, b11, trow1, b00, send, trow, group, tacc, wv, si, so):
    ins = copier(lambda j: w.at[j], lambda j: wv.at[j], si)
    start_all(Z, ins)
    size = CR + TE
    outs = [
        pltpu.make_async_copy(blk, group.at[pl.ds(q * size, size), :], so.at[q])
        for q, blk in enumerate((b00, b10))
    ]
    for copy in outs:
        copy.start()
    send[...] = jnp.zeros_like(send)
    tacc[...] = jnp.zeros_like(tacc)
    for j in range(Z):
        ins(j).wait()
        e_step(wv[j], (b10, b11), send, tacc)
    trow[...] = trow1[...]
    put_totals(s, 1, tacc, trow)
    send[2 * CR : 2 * CR + 16, :] = trow[...]
    for copy in outs:
        copy.wait()


def put_rows(racc, rsc):
    for k in range(8):
        rsc[k : k + 1, :] = racc[0:1, k * 256 : (k + 1) * 256]


def k_body(s, w, za, zb, epoch, after, kt, rz, racc, rsc):
    i = pl.program_id(0)

    @pl.when(i == 0)
    def _():
        racc[...] = jnp.zeros_like(racc)

    tau = 0.04 + 0.001 * epoch[0:1, 0:1].astype(F32)
    factor = LOG2E / tau
    wn, _ = unit(w[...])
    wb = wn.astype(BF16)
    half = NT // 2
    ka = jnp.exp2(dot(wb, za[...], 1, 1) * factor)
    kb = jnp.exp2(dot(wb, zb[...], 1, 1) * factor)
    kt[0, :, 0:half] = ka.astype(BF16)
    kt[0, :, half:NT] = kb.astype(BF16)
    c = 1.0 / (jnp.sum(ka, axis=1, keepdims=True) + jnp.sum(kb, axis=1, keepdims=True))
    racc[0:1, 0:half] += jnp.sum(ka * c, axis=0, keepdims=True)
    racc[0:1, half:NT] += jnp.sum(kb * c, axis=0, keepdims=True)

    @pl.when(i == pl.num_programs(0) - 1)
    def _():
        put_rows(racc, rsc)
        for b in range(Z):
            rz[b] = rsc[...]


def mid1_body(s, rz, tpk, tin, out):
    r = jnp.sum(rz[...], axis=0)
    ab = tpk[...] + tin[2 * CR : 2 * CR + 16, :]
    for b in range(C * NP):
        out[b, 0:8, :] = r
        out[b, 8:12, :] = ab[0:4]
        out[b, 12:16, :] = ab[8:12]


def mid2_body(s, rz, keep, tin, out, done, g):
    c = s[2]
    r = jnp.sum(rz[:, 0:8, :], axis=0)
    done[...] = jnp.zeros_like(done)
    g[...] = keep[...] + tin[0 : 2 * CR, :]
    for cd in range(C):
        for p in range(NP):
            out[cd * NP + p, 0:8, :] = r
            out[cd * NP + p, 8:40, :] = g[pl.ds((c ^ cd) * CR + p * 32, 32), :]


def row_total(s, got, sc):
    c = s[2]
    same = jnp.zeros((8, D), F32)
    other = jnp.zeros((8, D), F32)
    for p in range(NP):
        same = same + got[c * NP + p, 0:8, :]
        other = other + got[(1 - c) * NP + p, 0:8, :]
    sc[0:4, :] = same[0:4] + other[4:8]
    sc[4:8, :] = same[4:8] + other[0:4]


def scales(s, got, rsc, u):
    row_total(s, got, rsc)
    inv = 1.0 / rsc[...]
    for k in range(8):
        u[0:1, k * 256 : (k + 1) * 256] = inv[k : k + 1, :]


def it2_body(s, kt, got, rz, racc, rsc, u, a, kv, si):
    ins = copier(lambda k: kt.at[k], lambda k: kv.at[k], si)
    start_all(KC, ins)
    racc[...] = jnp.zeros_like(racc)
    scales(s, got, rsc, u)
    tot = jnp.sum(got[:, 8:16, :], axis=0)
    a[0:4, :] = tot[4:8] / tot[0:4]
    a[4:8, :] = tot[4:8]

    def step(j):
        ins(j).wait()
        k = kv[j].astype(F32)
        c = 1.0 / jnp.sum(k * u[...], axis=1, keepdims=True)
        racc[...] += jnp.sum(k * c, axis=0, keepdims=True)

    loop(KC, step)
    put_rows(racc, rsc)
    for b in range(Z):
        rz[b, 0:8, :] = rsc[...]
        rz[b, 8:16, :] = a[...]


def it3_body(s, kt, got, after, rz, ccol, racc, rsc, u, crow, kv, si):
    ins = copier(lambda k: kt.at[k], lambda k: kv.at[k], si)
    start_all(KC, ins)
    racc[...] = jnp.zeros_like(racc)
    crow[...] = jnp.zeros_like(crow)
    scales(s, got, rsc, u)

    def step(j):
        ins(j).wait()
        k = kv[j].astype(F32)
        ku = k * u[...]
        t = ku[:, 0:128]
        for a in range(1, NT // 128):
            t = t + ku[:, a * 128 : (a + 1) * 128]
        c = 1.0 / jnp.sum(t, axis=1, keepdims=True)
        ccol[j] = jnp.broadcast_to(c, (KR, 128))
        crow[pl.ds(j, 1), :] = 1.0 / jnp.sum(t.T, axis=0, keepdims=True)
        racc[...] += jnp.sum(k * c, axis=0, keepdims=True)

    loop(KC, step)
    put_rows(racc, rsc)
    for b in range(Z):
        rz[b, 0:8, :] = rsc[...]
        rz[b, 8:16, :] = crow[...]


def gw_body(s, w, h_own, h_other, rz, after, out, done, wb):
    yh, c = s[0], s[2]

    @pl.when(pl.program_id(0) == 0)
    def _():
        wn, _ = unit(w[...])
        wb[...] = wn.astype(BF16)
        out[...] = jnp.zeros_like(out)
        done[...] = jnp.zeros_like(done)

    for j in range(2):
        acc = None
        for q in range(4):
            zq = (h_own, h_other)[q % 2][j, (q // 2) * (CR + TE) : (q // 2) * (CR + TE) + CR, :]
            at = 8 + (yh ^ (q // 2)) * 2 + (c ^ (q % 2))
            a = rz[pl.program_id(0) * 2 + j, pl.ds(at, 1), :]
            e = jnp.exp2(dot(wb[...], zq, 1, 1) * (STUDENT * LOG2E)) * a
            part = dot(e.astype(BF16), zq)
            acc = part if acc is None else acc + part
        out[...] += acc


def cw_body(s, w, za, zb, epoch, rz, after, keep, send, zp, acc):
    i = pl.program_id(0)
    c = s[2]

    @pl.when(i == 0)
    def _():
        zp[0:TE, :] = za[...]
        zp[TE : 2 * TE, :] = zb[...]
        acc[...] = jnp.zeros_like(acc)

    factor = LOG2E / (0.04 + 0.001 * epoch[0:1, 0:1].astype(F32))
    part = None
    for j in range(CWS):
        wb = w[j]
        e = jnp.exp2(dot(zp[...], wb, 1, 1) * factor).astype(BF16).astype(F32)
        at = i * CWS + j
        yy, zz = at // Z, at % Z
        for h in range(2):
            row = rz[zz, pl.ds(8 + 2 * yy + h, 1), :]
            codes = (e[:, h * 256 : (h + 1) * 256] * row).astype(BF16)
            one = dot(codes, wb[h * 256 : (h + 1) * 256])
            part = one if part is None else part + one
    acc[...] += part

    @pl.when(i == pl.num_programs(0) - 1)
    def _():
        r = jnp.sum(rz[:, 0:8, :], axis=0)
        keep[0:8, :] = r
        keep[8 : 8 + TE, :] = acc[0:TE, :]
        send[0:4, :] = r[4:8]
        send[4:8, :] = r[0:4]
        send[8 : 8 + TE, :] = acc[TE : 2 * TE, :]


def mid3_body(s, keep, tin, got2, out):
    pack = keep[...] + tin[...]
    g = jnp.sum(got2[:, 8:40, :], axis=0)
    for p in range(NP):
        out[p, 0:72, :] = pack
        out[p, 72:104, :] = g


def last_body(
    s, sf, pairs, mask, got1, got3, kt, ccol, h_own, h_other, gwp, w,
    loss, feats, protos,
    rsc, trow, g, hv, kv, cv, u_all, si,
):
    n = KC // YH
    ks = copier(lambda k: kt.at[s[0] * n + k], lambda k: kv.at[k], si)
    start_all(n, ks)

    def crops(h, cc):
        def copy(at):
            block = (at // Z) ^ s[0]
            to = cc * YH * Z + at
            return pltpu.make_async_copy(
                h.at[at % Z, pl.ds(block * (CR + TE) + CR, TE), :],
                hv.at[pl.ds(to * TE, TE), :],
                si.at[n + to],
            )

        return copy

    crops_own, crops_other = crops(h_own, 0), crops(h_other, 1)
    start_all(YH * Z, crops_own)
    start_all(YH * Z, crops_other)
    more = pltpu.make_async_copy(ccol.at[pl.ds(s[0] * n, n)], cv, si.at[n + 32])
    more.start()

    yh, z, c = s[0], s[1], s[2]
    zs, inv = unit(sf[...])
    zsb = zs.astype(BF16).astype(F32)
    trow[...] = jnp.sum(got1[:, 8:16, :], axis=0)
    at = yh * 2 + c
    t = trow[pl.ds(at, 1), :]
    msum = trow[pl.ds(at + 4, 1), :]
    a = jnp.broadcast_to(msum / t, (128, CR)).T[:, 0:1]
    rsc[...] = 1.0 / jnp.sum(got3[:, 0:8, :], axis=0)
    own = yh * Z + z
    row = rsc[pl.ds(own // 4, 1), :]
    u = row[:, 0:128]
    u = jnp.where(own % 4 >= 2, row[:, 128:256], u)
    col = jnp.broadcast_to(u, (128, 128)).T
    ucol = jnp.where(own % 2 == 1, col[TE : 2 * TE, 0:1], col[0:TE, 0:1])
    cw = jnp.sum(got3[:, 8:72, :], axis=0) * ucol
    for p in range(NP):
        g[p * 32 : (p + 1) * 32, :] = got3[p, 72:104, :]
    q = dot(selector(pairs, mask), cw, 0, 0, lax.Precision.HIGHEST)
    cross = dot(jnp.ones((8, D), F32), zsb * q, 1, 1, lax.Precision.HIGHEST)
    loss[...] = msum * jnp.log(t) - STUDENT * cross[0:1, :]
    gz = SCALE * (a * g[...] - q)
    feats[...] = (gz - zs * jnp.sum(zs * gz, axis=1, keepdims=True)) * inv

    for k in range(8):
        u_all[0:1, k * D : (k + 1) * D] = rsc[k : k + 1, :]
    wait_all(YH * Z, crops_own)
    wait_all(YH * Z, crops_other)
    more.wait()

    def step(k):
        ks(k).wait()
        acc = dot((kv[k].astype(F32) * u_all[...]).astype(BF16), hv[...])
        rows = pl.ds(k * KR, KR)
        wn, inv_w = unit(w[rows, :])
        gw = SCALE * (gwp[rows, :] - acc * cv[k, :, 0:1])
        protos[rows, :] = (gw - wn * jnp.sum(wn * gw, axis=1, keepdims=True)) * inv_w

    loop(n, step)


def local(student, teacher, prototypes, pairs, mask, epoch):
    yh, z, c = lax.axis_index("yh"), lax.axis_index("z"), lax.axis_index("c")
    p = lax.axis_index(("yl", "x"))
    idx = jnp.stack([yh, z, c, p]).astype(jnp.int32)
    ep = epoch.reshape(1, 1)
    student, teacher, protos = hbm(student), hbm(teacher), hbm(prototypes)
    pairs, mask = hbm(pairs.T), hbm(mask.T)
    chunked = hbm(prototypes.reshape(YH * Z, C, SH, D))
    swap = [(0, 1), (1, 0)]
    prc = ("c", "yl", "x")

    spay, trep = call(
        prep_body, idx, 1,
        (student, teacher, pairs, mask),
        [whole((CR, D)), whole((TE, D)), whole((2, CR)), whole((2, CR))],
        [sds((CR + TE, D), BF16), sds((YH * Z, TE, D), BF16)],
        [whole((CR + TE, D)), whole((YH * Z, TE, D))],
        nbytes=1 << 20,
    )
    b00 = spay
    b01 = lax.ppermute(b00, "c", swap)
    b10 = lax.ppermute(b00, "yh", swap)
    za = lax.all_to_all(trep, ("yh", "z"), 0, 0, tiled=True).reshape(NT // 2, D)
    wbuf = pltpu.VMEM((Z, SH, D), BF16)
    tbuf = pltpu.VMEM((2 * CR, 128), F32)
    half = Z // 2
    pair_spec = spec((2, SH, D), lambda i, s: (i, 0, 0))
    keep, trow1, wnb = call(
        e1_body, idx, half,
        (chunked, b00, b01, mask),
        [spec((2, 1, SH, D), lambda i, s: (s[0] * half + i, s[2], 0, 0))]
        + [whole((CR + TE, D))] * 2
        + [whole((2, CR))],
        [sds((2 * CR, D), F32), sds((16, D), F32), pltpu.HBM((Z, SH, D), BF16)],
        [whole((2 * CR, D)), whole((16, D)), pair_spec],
        [tbuf], flops=4 << 30, nbytes=4 << 20,
    )
    b10, trow1 = lax.optimization_barrier((b10, trow1))
    b11 = lax.ppermute(b10, "c", swap)
    send, tpk, group = call(
        e2_body, idx, 1,
        (hbm(wnb), b10, b11, trow1, b00),
        [ANY] + [whole((CR + TE, D))] * 2 + [whole((16, D)), ANY],
        [sds((2 * CR + 16, D), F32), sds((16, D), F32), pltpu.HBM((2 * (CR + TE), D), BF16)],
        [whole((2 * CR + 16, D)), whole((16, D)), ANY],
        [tbuf, wbuf, sems(Z), sems(2)], flops=4 << 30, nbytes=4 << 20,
    )
    tin = lax.ppermute(send, "yh", swap)
    za, tpk, group = lax.optimization_barrier((za, tpk, group))
    h_own = lax.all_gather(group, "z", axis=0, tiled=False)
    zb = lax.ppermute(za, "c", swap)

    kbuf = pltpu.VMEM((KC, KR, NT), BF16)
    kt_spec = spec((1, KR, NT), lambda i, s: (i, 0, 0))
    per = SH // KR
    kt, rz1 = call(
        k_body, idx, KC,
        (protos, za, zb, ep, tpk),
        [
            spec((KR, D), lambda i, s: ((((i // per) * Z + s[1]) * C + s[2]) * per + i % per, 0)),
            whole((NT // 2, D)), whole((NT // 2, D)), whole((1, 1)), ANY,
        ],
        [
            pltpu.HBM((KC, KR, NT), BF16), sds((Z, 8, D), F32),
        ],
        [kt_spec, whole((Z, 8, D))],
        [pltpu.VMEM((1, NT), F32), pltpu.VMEM((8, D), F32)],
        flops=4 << 30, nbytes=10 << 20,
    )
    rz1 = lax.all_to_all(rz1, "z", 0, 0, tiled=True)
    pay1 = call(
        mid1_body, idx, 1,
        (rz1, tpk, tin),
        [whole((Z, 8, D)), whole((16, D)), whole((2 * CR + 16, D))],
        sds((C * NP, 16, D), F32), whole((C * NP, 16, D)),
        nbytes=1 << 19,
    )
    got1 = lax.all_to_all(pay1, prc, 0, 0, tiled=True)

    it_scratch = [pltpu.VMEM((1, NT), F32), pltpu.VMEM((8, D), F32), pltpu.VMEM((1, NT), F32)]
    rz2 = call(
        it2_body, idx, 1,
        (hbm(kt), got1),
        [ANY, whole((C * NP, 16, D))],
        sds((Z, 16, D), F32), whole((Z, 16, D)),
        it_scratch + [pltpu.VMEM((8, D), F32), kbuf, sems(KC)], nbytes=9 << 20,
    )
    rz2 = lax.all_to_all(rz2, "z", 0, 0, tiled=True)
    h_own, rz2 = lax.optimization_barrier((h_own, rz2))
    h_other = lax.ppermute(h_own, "c", swap)
    pay2, done2 = call(
        mid2_body, idx, 1,
        (rz2, keep, tin),
        [whole((Z, 16, D)), whole((2 * CR, D)), whole((2 * CR + 16, D))],
        [sds((C * NP, 40, D), F32), sds((8, 128), F32)],
        [whole((C * NP, 40, D)), whole((8, 128))],
        [pltpu.VMEM((2 * CR, D), F32)],
        nbytes=2 << 20,
    )
    gwp, done3 = call(
        gw_body, idx, half,
        (protos, hbm(h_own), hbm(h_other), rz2, done2),
        [
            spec((SH, D), lambda i, s: ((s[0] * Z + s[1]) * C + s[2], 0)),
            spec((2, 2 * (CR + TE), D), lambda i, s: (i, 0, 0)),
            spec((2, 2 * (CR + TE), D), lambda i, s: (i, 0, 0)),
            whole((Z, 16, D)), ANY,
        ],
        [sds((SH, D), F32), sds((8, 128), F32)],
        [whole((SH, D)), whole((8, 128))],
        [pltpu.VMEM((SH, D), BF16)],
        flops=8 << 30, nbytes=8 << 20,
    )
    got2 = lax.all_to_all(pay2, prc, 0, 0, tiled=True)
    rz3, ccol = call(
        it3_body, idx, 1,
        (hbm(kt), got2, done3),
        [ANY, whole((C * NP, 40, D)), ANY],
        [sds((Z, 16, D), F32), pltpu.HBM((KC, KR, 128), F32)],
        [whole((Z, 16, D)), whole((KC, KR, 128))],
        it_scratch + [pltpu.VMEM((8, D), F32), kbuf, sems(KC)], nbytes=9 << 20,
    )
    wall = pltpu.VMEM((YH * Z, SH, D), BF16)
    wnc, done = call(
        norm_body, idx, 1,
        (chunked, rz3),
        [ANY, ANY],
        [pltpu.HBM((YH * Z, SH, D), BF16), sds((8, 128), F32)],
        [ANY, whole((8, 128))],
        [wall, wall, sems(YH * Z), sems(YH * Z)],
        flops=2 << 30, nbytes=8 << 20,
    )
    rz3 = lax.all_to_all(rz3, "z", 0, 0, tiled=True)
    keep3, send3 = call(
        cw_body, idx, YH * Z // CWS,
        (hbm(wnc), za, zb, ep, rz3, done3),
        [
            spec((CWS, SH, D), lambda i, s: (i, 0, 0)),
            spec((TE, D), lambda i, s: (s[0] * Z + s[1], 0)),
            spec((TE, D), lambda i, s: (s[0] * Z + s[1], 0)),
            whole((1, 1)), whole((Z, 16, D)), ANY,
        ],
        [sds((8 + TE, D), F32)] * 2, [whole((8 + TE, D))] * 2,
        [pltpu.VMEM((2 * TE, D), BF16), pltpu.VMEM((2 * TE, D), F32)],
        flops=1 << 30, nbytes=6 << 20,
    )
    tin3 = lax.ppermute(send3, "c", swap)
    pay3 = call(
        mid3_body, idx, 1,
        (keep3, tin3, got2),
        [whole((8 + TE, D))] * 2 + [whole((C * NP, 40, D))],
        sds((NP, 104, D), F32), whole((NP, 104, D)),
        nbytes=2 << 20,
    )
    got3 = lax.all_to_all(pay3, ("yl", "x"), 0, 0, tiled=True)

    n = KC // YH
    loss, grad_feats, grad_proto = call(
        last_body, idx, 1,
        (student, pairs, mask, got1, got3, hbm(kt), hbm(ccol), hbm(h_own), hbm(h_other), gwp, protos),
        [
            whole((CR, D)), whole((2, CR)), whole((2, CR)),
            whole((C * NP, 16, D)), whole((NP, 104, D)),
            ANY, ANY, ANY, ANY, whole((SH, D)),
            spec((SH, D), lambda i, s: ((s[0] * Z + s[1]) * C + s[2], 0)),
        ],
        [sds((1, CR), F32), sds((CR, D), F32), sds((SH, D), F32)],
        [whole((1, CR)), whole((CR, D)), whole((SH, D))],
        [
            pltpu.VMEM((8, D), F32), pltpu.VMEM((8, D), F32), pltpu.VMEM((CR, D), F32),
            pltpu.VMEM((NT, D), BF16), pltpu.VMEM((n, KR, NT), BF16),
            pltpu.VMEM((n, KR, 128), F32), pltpu.VMEM((1, NT), F32), sems(n + 33),
        ],
        flops=1 << 30, nbytes=8 << 20,
    )
    return loss.reshape(CR), grad_feats, grad_proto


def solution(mesh):
    fine = Mesh(mesh.devices.reshape(YH, Z, C, YL, X), ("yh", "z", "c", "yl", "x"))
    dp, proto = ("yh", "z", "c"), ("yl", "x")
    in_specs = (P(dp, None), P(dp, None), P(proto, None), P(dp, None), P(dp, None), P())
    out_specs = (P(dp), P(dp, None), P(proto + dp, None))
    return jax.shard_map(local, mesh=fine, in_specs=in_specs, out_specs=out_specs, check_vma=False)
```
